256 devices in a mesh: band: 4 (over z_hi), fft: 64 (over x, z_lo, y, core).
Axes of the slice: x: 4, y: 4, z: 8 (z_hi: 4, z_lo: 2; z = z_hi * 2 + z_lo), core: 2. Of those that a mesh axis runs over, the one named last changes fastest.
Arguments:
- wave_coef: float32 [2, 8, 160, 8192], P(None, 'band', None, 'fft'), may hold values from -6 to 6
- stick_map: int32 [8192], P('fft'), may hold values from 0 to 25599, as said below
- local_potential: float32 [192, 25600], P('fft'), may hold values from -6 to 6
- core_density: float32 [192, 25600], P('fft'), may hold values from 0.05 to 1
- occupations: float32 [8], P('band'), may hold values from 0.5 to 2
- block_place: int32 [6144], P('fft'), may hold values from 0 to 599, as said below
- block_atom: int32 [6144], P('fft'), may hold values from 0 to 1023, as said below
- projectors: float32 [6144, 64, 128], P('fft'), may hold values from -0.5 to 0.5
- coupling: float32 [64, 64], replicated, may hold values from -0.75 to 0.75
Outputs:
- applied: float32 [2, 8, 160, 8192], P(None, 'band', None, 'fft')
- density: float32 [192, 25600], P('fft')
- exchange_field: float32 [192, 25600], P('fft')
The draws below stay inside these ranges and needn't reach their ends.
Inputs may be any that keep to these rules, and one draw needn't show every extreme that they name: `stick_map`: values are distinct; the 8192 sticks are the columns of smallest (x / 160)^2 + (y / 160)^2 in signed frequencies, ties in any order, placed along the array in any order. `block_place`: on fft index f the 96 entries never fall, lie in blocks of the slots s with s * 64 + f < 160, and the last is the last block of those slots. `block_atom`: on fft index f every entry is (f * 16 - 16 // 2 + i) mod 1024 for some i < 32, and each such atom appears there.
All inputs are finite; a program needn't handle non-finite values.
Results may differ from the reference program's by a relative error of at most 0.0001.
Values sent between devices are 32-bit elements; how exact they have to be, the bound alone decides.
A program may use at most 192 MiB of HBM per device.

```python
import math
import jax
import jax.numpy as jnp
from jax import lax

NX = 160
NY = 160
NZ = 160
NPROJ = 64
STICK_DEV = 128
ATOM_DEV = 16
NBLK = 96
BANDS = 8
STICKS = 8192
ATOMS = 1024
BLOCKS = 6144
ZP = 3
ZPLANES = 192
N_FFT = 64


def draw_stick_map(key, part):
    key = jax.random.fold_in(key, 11)
    order_key, spread_key = jax.random.split(key)
    columns = jnp.arange(NX * NY, dtype=jnp.int32)
    xfreq = columns // NY
    yfreq = columns % NY
    xfreq = jnp.where(xfreq < (NX + 1) // 2, xfreq, xfreq - NX)
    yfreq = jnp.where(yfreq < (NY + 1) // 2, yfreq, yfreq - NY)
    radius = xfreq * xfreq * (NY * NY) + yfreq * yfreq * (NX * NX)
    shuffle = jax.random.permutation(order_key, NX * NY).astype(jnp.int32)
    ranked = shuffle[jnp.argsort(radius[shuffle], stable=True)]
    chosen = ranked[:STICKS]
    placed = chosen[jax.random.permutation(spread_key, STICKS)]
    return placed.astype(jnp.int32)


def draw_block_place(key, part):
    key = jax.random.fold_in(key, 12)
    fft_count = STICKS // STICK_DEV
    plane_slots = (NZ + fft_count - 1) // fft_count
    device = jnp.arange(fft_count, dtype=jnp.int32)
    usable = jnp.clip((NZ - device + fft_count - 1) // fft_count, 1, plane_slots) * (NX * NY // 128)
    raw = jax.random.randint(key, (fft_count, NBLK), 0, 1 << 30, dtype=jnp.int32)
    placed = jnp.sort(raw % usable[:, None], axis=1)
    placed = placed.at[:, NBLK - 1].set(usable - 1)
    return placed.reshape(-1).astype(jnp.int32)


def draw_block_atom(key, part):
    key = jax.random.fold_in(key, 13)
    pick_key, mix_key = jax.random.split(key)
    fft_count = STICKS // STICK_DEV
    window = 2 * ATOM_DEV
    position = jnp.arange(NBLK, dtype=jnp.int32)
    picked = jax.random.randint(pick_key, (fft_count, NBLK), 0, window, dtype=jnp.int32)
    offsets = jnp.where(position[None, :] < window, position[None, :] % window, picked)
    mixed = jax.vmap(jax.random.permutation)(jax.random.split(mix_key, fft_count), offsets)
    device = jnp.arange(fft_count, dtype=jnp.int32)[:, None]
    atoms = (device * ATOM_DEV - ATOM_DEV // 2 + mixed) % (ATOM_DEV * fft_count)
    return atoms.reshape(-1).astype(jnp.int32)


def block_scale(stream_key, dims, shards, smallest, top_value):
    factor_of, own = 1.0, jax.random.fold_in(stream_key, 6)
    for dim, shards_of in shards:
        heights = jnp.exp(jax.random.uniform(jax.random.fold_in(own, dim), (shards_of,), jnp.float32, smallest / len(shards), top_value / len(shards)))
        factor_of = factor_of * jnp.repeat(heights, dims[dim] // shards_of).reshape([-1 if axis == dim else 1 for axis in range(len(dims))])
    return factor_of


def centred(own_key, dims, scale, reach, cuts=(), kind=jnp.bfloat16):
    drawn = jax.random.normal(own_key, dims, jnp.float32) * scale
    if len(cuts) > 0:
        drawn = block_scale(own_key, dims, cuts, -0.22, 0.18) * drawn
    return jnp.clip(drawn, min=-reach, max=reach).astype(kind)


def setup_inputs(seed: int = 0) -> dict:
    splits = jax.random.split(jax.random.key(seed), 10)
    wave_coef = centred(splits[0], (2, BANDS, NZ, STICKS), 1.0, 6.0, ((1, 4), (3, 64)), jnp.float32)
    stick_map = draw_stick_map(jax.random.fold_in(splits[9], 71), 0)
    local_potential = centred(splits[2], (ZPLANES, NX * NY), 1.0, 6.0, ((0, 64),), jnp.float32)
    core_density = jnp.clip(jnp.exp(math.log(1.0) - 2.9957323 * jax.random.uniform(splits[3], (ZPLANES, NX * NY), jnp.float32) ** block_scale(splits[3], (ZPLANES, NX * NY), ((0, 64),), -0.2, 0.2)), 0.05, 1.0)
    occupations = jnp.clip(0.5 + 1.5 * jax.random.uniform(splits[4], (BANDS,), jnp.float32) ** block_scale(splits[4], (BANDS,), ((0, 4),), -0.2, 0.2), 0.5, 2.0)
    block_place = draw_block_place(jax.random.fold_in(splits[9], 71), 0)
    block_atom = draw_block_atom(jax.random.fold_in(splits[9], 71), 0)
    projectors = centred(splits[7], (BLOCKS, NPROJ, 128), 128 ** -0.5, 0.5, ((0, 64),), jnp.float32)
    coupling = centred(splits[8], (NPROJ, NPROJ), NPROJ ** -0.5, 0.75, (), jnp.float32)
    return dict(wave_coef=wave_coef, stick_map=stick_map, local_potential=local_potential, core_density=core_density, occupations=occupations, block_place=block_place, block_atom=block_atom, projectors=projectors, coupling=coupling)


lda_factor = (3.0 / math.pi) ** (1.0 / 3.0)


def folded(index, count):
    return jnp.where(index < (count + 1) // 2, index, index - count)


def reference(wave_coef, stick_map, local_potential, core_density, occupations, block_place, block_atom, projectors, coupling):
    highest = lax.Precision.HIGHEST
    ftype = wave_coef.dtype
    slots = jnp.arange(ZPLANES, dtype=jnp.int32)
    zplane = (slots % ZP) * N_FFT + slots // ZP
    validf = (zplane < NZ).astype(ftype)
    zclip = jnp.minimum(zplane, NZ - 1)
    xfreq = folded(stick_map // NY, NX).astype(ftype) / NX
    yfreq = folded(stick_map % NY, NY).astype(ftype) / NY
    zfreq = folded(jnp.arange(NZ, dtype=jnp.int32), NZ).astype(ftype) / NZ
    kinetic = 2.0 * (xfreq * xfreq + yfreq * yfreq)[None, :] + 2.0 * (zfreq * zfreq)[:, None]
    owner = jnp.arange(BLOCKS, dtype=jnp.int32) // NBLK
    global_block = owner * (ZP * NX * NY // 128) + block_place
    block_total = ZPLANES * NX * NY // 128

    def one_band(density, band_in):
        pair, weight = band_in
        coef = pair[0] + 1j * pair[1]
        full = jnp.zeros((NZ, NX * NY), coef.dtype).at[:, stick_map].set(coef)
        real_grid = jnp.fft.ifftn(full.reshape(NZ, NX, NY), norm="ortho")
        planes = real_grid[zclip].reshape(ZPLANES, NX * NY)
        part_re = jnp.real(planes) * validf[:, None]
        part_im = jnp.imag(planes) * validf[:, None]
        stacked = jnp.stack([part_re, part_im])
        pieces = stacked.reshape(2, block_total, 128)[:, global_block, :]
        project = jnp.einsum('kjp,ckp->kcj', projectors, pieces, precision=highest)
        summed = jax.ops.segment_sum(project, block_atom, num_segments=ATOMS)
        picked = summed[block_atom]
        weights = jnp.einsum('kcj,ij->kci', picked, coupling, precision=highest)
        added = jnp.einsum('kip,kci->ckp', projectors, weights, precision=highest)
        result = (local_potential[None] * stacked).reshape(2, block_total, 128)
        result = result.at[:, global_block, :].add(added).reshape(2, ZPLANES, NX * NY)
        result = result * validf[None, :, None]
        hgrid = jnp.zeros((NZ, NX * NY), coef.dtype).at[zclip].add(result[0] + 1j * result[1])
        spectrum = jnp.fft.fftn(hgrid.reshape(NZ, NX, NY), norm="ortho").reshape(NZ, NX * NY)[:, stick_map]
        out_re = jnp.real(spectrum) + kinetic * pair[0]
        out_im = jnp.imag(spectrum) + kinetic * pair[1]
        density = density + weight * (part_re * part_re + part_im * part_im)
        return density, jnp.stack([out_re, out_im])

    start = jnp.zeros((ZPLANES, NX * NY), ftype)
    density, applied = lax.scan(one_band, start, (jnp.transpose(wave_coef, (1, 0, 2, 3)), occupations))
    applied = jnp.transpose(applied, (1, 0, 2, 3))
    exchange_field = -lda_factor * jnp.cbrt(density + core_density) * validf[:, None]
    return applied, density, exchange_field
```

```python
import math

import jax
import jax.numpy as jnp
import numpy as np
from jax import lax
from jax.experimental import pallas as pl
from jax.experimental.pallas import tpu as pltpu
from jax.sharding import PartitionSpec as P

N = 160
ZP = 3
N_FFT = 64
NBLK = 96
ATOM_DEV = 16
ATOMS = 1024
SHIFT = 52
BOX = 104
HALF = 56
F32 = jnp.float32
BF16 = jnp.bfloat16

lda_factor = (3.0 / math.pi) ** (1.0 / 3.0)


def parts(table):
    high = table.astype(np.float32).astype(jnp.bfloat16)
    low = (table - high.astype(np.float64)).astype(np.float32).astype(jnp.bfloat16)
    return high, low


def real_form(cosine, sine):
    return np.block([[cosine, -sine], [sine, cosine]])


def z_tables():
    slot, place = np.meshgrid(np.arange(8), np.arange(N_FFT), indexing="ij")
    out = np.zeros((N_FFT, 8, 2, N))
    g = np.arange(N)
    for f in range(N_FFT):
        for s in range(ZP):
            z = s * N_FFT + f
            if z < N:
                phase = 2 * np.pi / N * ((z * g) % N)
                c, d = np.cos(phase) / math.sqrt(N), np.sin(phase) / math.sqrt(N)
                out[f, s, 0], out[f, s, 1] = c, -d
                out[f, 3 + s, 0], out[f, 3 + s, 1] = d, c
    forward = out.reshape(N_FFT * 8, 2 * N)
    return forward, forward.T


def x_tables():
    rows = np.array([4 * k + g for g in range(4) for k in range(40)])
    compact = np.array([2 * h + p for p in range(2) for h in range(HALF)])
    phase = 2 * np.pi / N * ((rows[:, None] * (compact[None, :] - SHIFT)) % N)
    keep = (compact < BOX)[None, :] / math.sqrt(N)
    ahead = real_form(np.cos(phase) * keep, np.sin(phase) * keep)
    compact = np.arange(BOX)
    phase = 2 * np.pi / N * (((compact[:, None] - SHIFT) * rows[None, :]) % N)
    back = real_form(np.cos(phase) / math.sqrt(N), -np.sin(phase) / math.sqrt(N))
    return ahead, back


PAIRS = tuple((j, g) for g in range(4) for j in (g, g + 1))


def y_tables():
    compact = np.arange(128)
    out = []
    for j, g in PAIRS:
        flat = 128 * j + np.arange(128)
        keep = ((flat // N == g)[None, :] & (compact < BOX)[:, None]) / math.sqrt(N)
        phase = 2 * np.pi / N * (((compact[:, None] - SHIFT) * (flat % N)[None, :]) % N)
        c, d = np.cos(phase) * keep, np.sin(phase) * keep
        out.append(np.block([[c, d], [-d, c]]))
    return np.stack(out)


def stack3(table, axis):
    high, low = parts(table)
    return np.concatenate([high, low, high], axis=axis)


def make_tables():
    z_ahead, z_back = z_tables()
    x_ahead, x_back = x_tables()
    y_ahead = y_tables()
    y_back = np.swapaxes(y_ahead, 1, 2)
    return dict(
        z_ahead=stack3(z_ahead, 1),
        z_back=stack3(z_back, 1),
        x_ahead=stack3(x_ahead, 1),
        x_back=stack3(x_back, 1),
        y_ahead=np.stack(parts(y_ahead), axis=1),
        y_back=np.stack(parts(y_back), axis=1),
    )


def split(value):
    high = value.astype(BF16)
    return high, (value - high.astype(F32)).astype(BF16)


def dot(left, right):
    return lax.dot_general(left, right, (((1,), (0,)), ((), ())), preferred_element_type=F32)


def dot_nt(left, right):
    return lax.dot_general(left, right, (((1,), (1,)), ((), ())), preferred_element_type=F32)


def lhs3(value):
    high, low = split(value)
    return jnp.concatenate([high, high, low], axis=1)


def rhs3(value):
    high, low = split(value)
    return jnp.concatenate([high, high, low], axis=0)


def grid_xy(stick_ref):
    column = stick_ref[...].astype(F32)
    x = jnp.floor((column + 0.5) * (1.0 / N))
    y = column - N * x
    return x, y


def block_row(place):
    slot = (place >= 200).astype(jnp.int32) + (place >= 400).astype(jnp.int32)
    inside = place - 200 * slot
    fifth = (inside * 6554) >> 15
    return slot * 200 + (inside - 5 * fifth) * 40 + fifth


def z_forward(stick_ref, wave_ref, table_ref, out_ref):
    x, y = grid_xy(stick_ref)
    half = N // 2
    xc = jnp.where(x < half, x, x - N) + SHIFT
    yc = jnp.where(y < half, y, y - N) + SHIFT
    both = [jnp.concatenate([wave_ref[0, b], wave_ref[1, b]], axis=0) for b in range(2)]
    result = dot(table_ref[...], rhs3(jnp.concatenate(both, axis=1)))
    for b in range(2):
        out_ref[:, 8 * b : 8 * b + 8, :] = result[:, 128 * b : 128 * b + 128].reshape(N_FFT, 8, 128)
    out_ref[:, 6:7, :] = jnp.broadcast_to(xc[None], (N_FFT, 1, 128))
    out_ref[:, 7:8, :] = jnp.broadcast_to(yc[None], (N_FFT, 1, 128))


def z_backward(stick_ref, wave_ref, table_ref, back_ref, out_ref):
    both = [back_ref[:, 8 * b : 8 * b + 8, :].reshape(N_FFT * 8, 128) for b in range(2)]
    result = dot(table_ref[...], rhs3(jnp.concatenate(both, axis=1)))
    x, y = grid_xy(stick_ref)
    half = N // 2
    x = jnp.where(x < half, x, x - N) / N
    y = jnp.where(y < half, y, y - N) / N
    g = lax.broadcasted_iota(jnp.int32, (N, 128), 0)
    z = jnp.where(g < half, g, g - N).astype(F32) / N
    kinetic = 2.0 * (x * x + y * y) + 2.0 * (z * z)
    for o in range(2):
        for b in range(2):
            spectrum = result[N * o : N * o + N, 128 * b : 128 * b + 128]
            out_ref[o, b] = spectrum + kinetic * wave_ref[o, b]


ROWS = [(b, o, s) for b in range(2) for o in range(2) for s in range(ZP)]
CHUNK = 4


def to_planes(
    place_ref,
    atom_ref,
    occ_ref,
    sticks_ref,
    xtab_ref,
    ytab_hbm,
    proj_hbm,
    psi_ref,
    sums_ref,
    dens_ref,
    grid_ref,
    mid_ref,
    ytab_ref,
    proj_ref,
    acc_ref,
    power_ref,
    sems,
):
    ytab_copy = pltpu.make_async_copy(ytab_hbm, ytab_ref, sems.at[0])
    proj_copy = pltpu.make_async_copy(proj_hbm, proj_ref, sems.at[1])
    ytab_copy.start()
    proj_copy.start()

    grid_ref[...] = jnp.zeros_like(grid_ref)
    row_id = lax.broadcasted_iota(jnp.int32, (HALF, 128), 0).astype(F32)
    lane_id = lax.broadcasted_iota(jnp.int32, (256, 128), 0).astype(F32)

    def scatter(chunk, carry):
        lefts, rights = [], []
        for i in range(CHUNK):
            tile = sticks_ref[chunk * CHUNK + i]
            x, y = tile[6:7], tile[7:8]
            x2 = jnp.floor(x * 0.5)
            here = row_id == x2
            spot = (lane_id == (x - 2.0 * x2) * 128.0 + y).astype(F32).astype(BF16)
            high = tile.astype(BF16).astype(F32)
            low = tile - high
            for piece in (high, low):
                picked = [
                    jnp.where(here, piece[8 * b + 3 * o + s : 8 * b + 3 * o + s + 1], 0.0)
                    for b, o, s in ROWS
                ]
                lefts.append(jnp.concatenate(picked, axis=0).astype(BF16))
                rights.append(spot)
        grid_ref[...] += dot_nt(jnp.concatenate(lefts, axis=1), jnp.concatenate(rights, axis=1))
        return carry

    lax.fori_loop(0, N_FFT // CHUNK, scatter, 0)

    columns = []
    for b in range(2):
        for s in range(ZP):
            rows = []
            for o in range(2):
                first = (b * 6 + o * 3 + s) * HALF
                for parity in range(2):
                    rows.append(
                        grid_ref[first : first + HALF, 128 * parity : 128 * parity + 128]
                    )
            columns.append(jnp.concatenate(rows, axis=0))
    mixed = dot(xtab_ref[...], rhs3(jnp.concatenate(columns, axis=1)))
    for g in range(4):
        for o in range(2):
            first = (o * 4 + g) * 40
            for bs in range(6):
                mid_ref[g, 40 * bs : 40 * bs + 40, 128 * o : 128 * o + 128] = mixed[
                    first : first + 40, 128 * bs : 128 * bs + 128
                ]
    lefts = [lhs3(mid_ref[g]) for g in range(4)]
    ytab_copy.wait()
    for j in range(5):
        total = None
        for at, (tile, g) in enumerate(PAIRS):
            if tile == j:
                high, low = ytab_ref[at, 0], ytab_ref[at, 1]
                term = dot(lefts[g], jnp.concatenate([high, low, high], axis=0))
                total = term if total is None else total + term
        for b in range(2):
            for s in range(ZP):
                bs = b * ZP + s
                for o in range(2):
                    first = s * 200 + j * 40
                    psi_ref[b * 2 + o, first : first + 40, :] = total[
                        40 * bs : 40 * bs + 40, 128 * o : 128 * o + 128
                    ]

    def power(b):
        re, im = psi_ref[2 * b], psi_ref[2 * b + 1]
        return re * re + im * im

    power_ref[...] = (occ_ref[0] * power(0) + occ_ref[1] * power(1)).reshape(ZP, 200, 128)
    for q in range(200):
        row = (q % 5) * 40 + q // 5
        dens_ref[:, 128 * q : 128 * q + 128] = power_ref[:, row, :]

    acc_ref[...] = jnp.zeros_like(acc_ref)
    base = lax.axis_index("fft") * ATOM_DEV - ATOM_DEV // 2
    proj_copy.wait()

    def project(k, carry):
        row = block_row(place_ref[k])
        first = ((atom_ref[k] - base) & (ATOMS - 1)) * 4
        values = proj_ref[k]
        for c in range(4):
            acc_ref[first + c] += values * psi_ref[c, pl.ds(row, 1), :]
        return carry

    lax.fori_loop(0, NBLK, project, 0)
    ones = jnp.ones((256, 128), BF16)
    lane = lax.broadcasted_iota(jnp.int32, (64, 128), 1)
    sums = jnp.zeros((64, 128), F32)
    for chunk in range(8):
        high, low = split(acc_ref[16 * chunk : 16 * chunk + 16].reshape(1024, 128))
        total = dot(jnp.concatenate([high, low], axis=1), ones)
        for m in range(16):
            sums = jnp.where(lane == chunk * 16 + m, total[64 * m : 64 * m + 64], sums)
    sums_ref[...] = sums


def to_sticks(
    place_ref,
    atom_ref,
    sums_ref,
    before_ref,
    after_ref,
    coupling_ref,
    sticks_ref,
    psi_ref,
    potential_ref,
    xtab_ref,
    ytab_hbm,
    proj_hbm,
    out_ref,
    weight_ref,
    pot_ref,
    h_ref,
    plane_ref,
    left_ref,
    ytab_ref,
    proj_ref,
    sems,
):
    ytab_copy = pltpu.make_async_copy(ytab_hbm, ytab_ref, sems.at[0])
    proj_copy = pltpu.make_async_copy(proj_hbm, proj_ref, sems.at[1])
    proj_copy.start()
    ytab_copy.start()

    for q in range(200):
        row = (q % 5) * 40 + q // 5
        pot_ref[:, row, :] = potential_ref[:, 128 * q : 128 * q + 128]
    potential = pot_ref[...].reshape(600, 128)
    for c in range(4):
        h_ref[c] = potential * psi_ref[c]

    lane = lax.broadcasted_iota(jnp.int32, (64, 128), 1)
    beside = jnp.where(
        lane < 64, pltpu.roll(before_ref[...], 64, 1), pltpu.roll(after_ref[...], 64, 1)
    )
    combined = sums_ref[...] + beside
    weight = lax.dot_general(
        coupling_ref[...],
        combined,
        (((1,), (0,)), ((), ())),
        precision=lax.Precision.HIGHEST,
        preferred_element_type=F32,
    )
    for n in range(128):
        weight_ref[n] = jnp.broadcast_to(weight[:, n : n + 1], (64, 128))
    base = lax.axis_index("fft") * ATOM_DEV - ATOM_DEV // 2
    proj_copy.wait()

    def add(k, carry):
        row = block_row(place_ref[k])
        first = ((atom_ref[k] - base) & (ATOMS - 1)) * 4
        values = proj_ref[k]
        for c in range(4):
            h_ref[c, pl.ds(row, 1), :] += jnp.sum(
                values * weight_ref[first + c], axis=0, keepdims=True
            )
        return carry

    lax.fori_loop(0, NBLK, add, 0)

    lefts = []
    for j in range(5):
        rows = []
        for b in range(2):
            for s in range(ZP):
                first = s * 200 + j * 40
                rows.append(
                    jnp.concatenate(
                        [h_ref[b * 2 + o, first : first + 40, :] for o in range(2)], axis=1
                    )
                )
        lefts.append(lhs3(jnp.concatenate(rows, axis=0)))
    ytab_copy.wait()
    turned = []
    for g in range(4):
        total = None
        for at, (j, group) in enumerate(PAIRS):
            if group == g:
                high, low = ytab_ref[at, 0], ytab_ref[at, 1]
                term = dot(lefts[j], jnp.concatenate([high, low, high], axis=0))
                total = term if total is None else total + term
        turned.append(total)
    columns = []
    for bs in range(6):
        rows = []
        for o in range(2):
            for g in range(4):
                rows.append(turned[g][40 * bs : 40 * bs + 40, 128 * o : 128 * o + 128])
        columns.append(jnp.concatenate(rows, axis=0))
    spectrum = dot(xtab_ref[...], rhs3(jnp.concatenate(columns, axis=1)))
    for at, (b, o, s) in enumerate(ROWS):
        bs = b * ZP + s
        plane_ref[at * BOX : at * BOX + BOX, :] = spectrum[
            o * BOX : o * BOX + BOX, 128 * bs : 128 * bs + 128
        ]
    high, low = split(plane_ref[...])
    left_ref[:, :128] = high
    left_ref[:, 128:] = low

    row_id = lax.broadcasted_iota(jnp.int32, (128, 256), 0).astype(F32)
    zeros = jnp.zeros((2, 256), F32)

    def gather(pair, carry):
        one, two = sticks_ref[2 * pair], sticks_ref[2 * pair + 1]
        x = jnp.concatenate([one[6:7], two[6:7]], axis=1)
        y = jnp.concatenate([one[7:8], two[7:8]], axis=1)
        spot = (row_id == y).astype(F32).astype(BF16)
        values = dot(left_ref[...], jnp.concatenate([spot, spot], axis=0))
        here = row_id[:BOX] == x
        rows = []
        for at in range(12):
            masked = jnp.where(here, values[at * BOX : at * BOX + BOX], 0.0)
            rows.append(jnp.sum(masked, axis=0, keepdims=True))
            if at % 6 == 5:
                rows.append(zeros)
        result = jnp.concatenate(rows, axis=0)
        out_ref[2 * pair] = result[:, :128]
        out_ref[2 * pair + 1] = result[:, 128:]
        return carry

    lax.fori_loop(0, N_FFT // 2, gather, 0)


VMEM = pltpu.VMEM
SMEM_SPEC = pl.BlockSpec(memory_space=pltpu.SMEM)
VMEM_SPEC = pl.BlockSpec(memory_space=pltpu.VMEM)
ANY_SPEC = pl.BlockSpec(memory_space=pl.ANY)
LIMIT = 56 * 1024 * 1024


def call(body, in_specs, outs, scratch=(), flops=0, size=0):
    return pl.pallas_call(
        body,
        out_shape=outs,
        in_specs=in_specs,
        out_specs=jax.tree.map(lambda _: VMEM_SPEC, outs),
        scratch_shapes=list(scratch),
        compiler_params=pltpu.CompilerParams(vmem_limit_bytes=LIMIT),
        cost_estimate=pl.CostEstimate(flops=flops, bytes_accessed=size, transcendentals=0),
    )


def shape(*dims):
    return jax.ShapeDtypeStruct(dims, F32)


def make_calls():
    forward = call(z_forward, [VMEM_SPEC] * 3, shape(N_FFT, 16, 128), (), 500_000_000, 2_000_000)
    backward = call(z_backward, [VMEM_SPEC] * 4, shape(2, 2, N, 128), (), 500_000_000, 2_000_000)
    planes = call(
        to_planes,
        [SMEM_SPEC] * 3 + [VMEM_SPEC] * 2 + [ANY_SPEC] * 2,
        (shape(4, 600, 128), shape(64, 128), shape(ZP, N * N)),
        (
            VMEM((12 * HALF, 256), F32),
            VMEM((4, 240, 256), F32),
            VMEM((8, 2, 256, 256), BF16),
            VMEM((NBLK, 64, 128), F32),
            VMEM((128, 64, 128), F32),
            VMEM((ZP, 200, 128), F32),
            pltpu.SemaphoreType.DMA((2,)),
        ),
        10_000_000_000,
        8_000_000,
    )
    sticks = call(
        to_sticks,
        [SMEM_SPEC] * 2 + [VMEM_SPEC] * 8 + [ANY_SPEC] * 2,
        shape(N_FFT, 16, 128),
        (
            VMEM((128, 64, 128), F32),
            VMEM((ZP, 200, 128), F32),
            VMEM((4, 600, 128), F32),
            VMEM((12 * BOX, 128), F32),
            VMEM((12 * BOX, 256), BF16),
            VMEM((8, 2, 256, 256), BF16),
            VMEM((NBLK, 64, 128), F32),
            pltpu.SemaphoreType.DMA((2,)),
        ),
        10_000_000_000,
        8_000_000,
    )
    return forward, backward, planes, sticks


def local(
    tables,
    wave_coef,
    stick_map,
    local_potential,
    core_density,
    occupations,
    block_place,
    block_atom,
    projectors,
    coupling,
):
    forward, backward, planes, sticks = make_calls()
    fft_index = lax.axis_index("fft")
    stick_row = stick_map.reshape(1, 128)
    sent = forward(stick_row, wave_coef, tables["z_ahead"])
    arrived = lax.all_to_all(sent, "fft", split_axis=0, concat_axis=0, tiled=True)
    psi, sums, group_density = planes(
        block_place,
        block_atom,
        occupations,
        arrived,
        tables["x_ahead"],
        tables["y_ahead"],
        projectors,
    )
    density = lax.psum(group_density, "band")
    up = [(i, (i + 1) % N_FFT) for i in range(N_FFT)]
    down = [(j, i) for i, j in up]
    before = lax.ppermute(sums, "fft", up)
    after = lax.ppermute(sums, "fft", down)
    result = sticks(
        block_place,
        block_atom,
        sums,
        before,
        after,
        coupling,
        arrived,
        psi,
        local_potential,
        tables["x_back"],
        tables["y_back"],
        projectors,
    )
    returned = lax.all_to_all(result, "fft", split_axis=0, concat_axis=0, tiled=True)
    applied = backward(stick_row, wave_coef, tables["z_back"], returned)
    valid = (jnp.arange(ZP, dtype=jnp.int32) * N_FFT + fft_index < N).astype(F32)
    exchange_field = -lda_factor * jnp.cbrt(density + core_density) * valid[:, None]
    return (applied, density, exchange_field)


def solution(mesh):
    tables = {name: jnp.asarray(value) for name, value in make_tables().items()}

    def run(*args):
        return local(tables, *args)

    return jax.shard_map(
        run,
        mesh=mesh,
        in_specs=(
            P(None, "band", None, "fft"),
            P("fft"),
            P("fft", None),
            P("fft", None),
            P("band"),
            P("fft"),
            P("fft"),
            P("fft", None, None),
            P(),
        ),
        out_specs=(P(None, "band", None, "fft"), P("fft", None), P("fft", None)),
        check_vma=False,
    )
```

```python
import math

import jax
import jax.numpy as jnp
import numpy as np
from jax import lax
from jax.experimental import pallas as pl
from jax.experimental.pallas import tpu as pltpu
from jax.sharding import PartitionSpec as P

N = 160
ZP = 3
N_FFT = 64
NBLK = 96
ATOM_DEV = 16
ATOMS = 1024
BANDS_AXIS = 4
SLICE = 152
SHIFT = 52
BOX = 104
HALF = 56
F32 = jnp.float32
BF16 = jnp.bfloat16

lda_factor = (3.0 / math.pi) ** (1.0 / 3.0)


def parts(table):
    high = table.astype(np.float32).astype(jnp.bfloat16)
    low = (table - high.astype(np.float64)).astype(np.float32).astype(jnp.bfloat16)
    return high, low


def real_form(cosine, sine):
    return np.block([[cosine, -sine], [sine, cosine]])


def z_tables():
    slot, place = np.meshgrid(np.arange(8), np.arange(N_FFT), indexing="ij")
    out = np.zeros((N_FFT, 8, 2, N))
    g = np.arange(N)
    for f in range(N_FFT):
        for s in range(ZP):
            z = s * N_FFT + f
            if z < N:
                phase = 2 * np.pi / N * ((z * g) % N)
                c, d = np.cos(phase) / math.sqrt(N), np.sin(phase) / math.sqrt(N)
                out[f, s, 0], out[f, s, 1] = c, -d
                out[f, 3 + s, 0], out[f, 3 + s, 1] = d, c
    forward = out.reshape(N_FFT * 8, 2 * N)
    return forward, forward.T


def x_tables():
    rows = np.array([4 * k + g for g in range(4) for k in range(40)])
    compact = np.array([2 * h + p for p in range(2) for h in range(HALF)])
    phase = 2 * np.pi / N * ((rows[:, None] * (compact[None, :] - SHIFT)) % N)
    keep = (compact < BOX)[None, :] / math.sqrt(N)
    ahead = real_form(np.cos(phase) * keep, np.sin(phase) * keep)
    compact = np.arange(BOX)
    phase = 2 * np.pi / N * (((compact[:, None] - SHIFT) * rows[None, :]) % N)
    back = real_form(np.cos(phase) / math.sqrt(N), -np.sin(phase) / math.sqrt(N))
    return ahead, back


PAIRS = tuple((j, g) for g in range(4) for j in (g, g + 1))


def y_tables():
    compact = np.arange(128)
    out = []
    for j, g in PAIRS:
        flat = 128 * j + np.arange(128)
        keep = ((flat // N == g)[None, :] & (compact < BOX)[:, None]) / math.sqrt(N)
        phase = 2 * np.pi / N * (((compact[:, None] - SHIFT) * (flat % N)[None, :]) % N)
        c, d = np.cos(phase) * keep, np.sin(phase) * keep
        out.append(np.block([[c, d], [-d, c]]))
    return np.stack(out)


def stack3(table, axis):
    high, low = parts(table)
    return np.concatenate([high, low, high], axis=axis)


def make_tables():
    z_ahead, z_back = z_tables()
    x_ahead, x_back = x_tables()
    y_ahead = y_tables()
    y_back = np.swapaxes(y_ahead, 1, 2)
    return dict(
        z_ahead=stack3(z_ahead, 1),
        z_back=stack3(z_back, 1),
        x_ahead=stack3(x_ahead, 1),
        x_back=stack3(x_back, 1),
        y_ahead=np.stack(parts(y_ahead), axis=1),
        y_back=np.stack(parts(y_back), axis=1),
    )


def split(value):
    high = value.astype(BF16)
    return high, (value - high.astype(F32)).astype(BF16)


def dot(left, right):
    return lax.dot_general(left, right, (((1,), (0,)), ((), ())), preferred_element_type=F32)


def dot_nt(left, right):
    return lax.dot_general(left, right, (((1,), (1,)), ((), ())), preferred_element_type=F32)


def lhs3(value):
    high, low = split(value)
    return jnp.concatenate([high, high, low], axis=1)


def rhs3(value):
    high, low = split(value)
    return jnp.concatenate([high, high, low], axis=0)


def grid_xy(stick_ref):
    column = stick_ref[...].astype(F32)
    x = jnp.floor((column + 0.5) * (1.0 / N))
    y = column - N * x
    return x, y


def block_row(place):
    slot = (place >= 200).astype(jnp.int32) + (place >= 400).astype(jnp.int32)
    inside = place - 200 * slot
    fifth = (inside * 6554) >> 15
    return slot * 200 + (inside - 5 * fifth) * 40 + fifth


def shifted(me, step, sign):
    def digit(value, unit, size):
        return lax.rem(lax.div(value, unit), size)

    core = lax.rem(digit(me, 1, 2) + digit(step, 1, 2), 2)
    y = lax.rem(digit(me, 2, 4) + sign * digit(step, 2, 4) + 4, 4)
    z = lax.rem(digit(me, 8, 2) + digit(step, 8, 2), 2)
    x = lax.rem(digit(me, 16, 4) + sign * digit(step, 16, 4) + 4, 4)
    return ((x * 2 + z) * 4 + y) * 2 + core


ROWS = [(b, o, s) for b in range(2) for o in range(2) for s in range(ZP)]
CHUNK = 4


def exchange_copy(send_ref, land_ref, send_sems, recv_sems, me, step):
    target = shifted(me, step, 1)
    return pltpu.make_async_remote_copy(
        src_ref=send_ref.at[target],
        dst_ref=land_ref.at[me],
        send_sem=send_sems.at[step],
        recv_sem=recv_sems.at[step],
        device_id={"fft": target},
        device_id_type=pl.DeviceIdType.MESH,
    )


def landing(send_ref, land_ref, send_sems, recv_sems, me, step):
    source = shifted(me, step, -1)
    return pltpu.make_async_remote_copy(
        src_ref=send_ref.at[source],
        dst_ref=land_ref.at[source],
        send_sem=send_sems.at[step],
        recv_sem=recv_sems.at[step],
        device_id={"fft": source},
        device_id_type=pl.DeviceIdType.MESH,
    )


def greet(barrier, me):
    def one(step, carry):
        pl.semaphore_signal(
            barrier,
            inc=1,
            device_id={"fft": shifted(me, step, 1)},
            device_id_type=pl.DeviceIdType.MESH,
        )
        return carry

    lax.fori_loop(1, N_FFT, one, 0)


def to_planes(
    occ_ref,
    stick_ref,
    wave_hbm,
    ztab_hbm,
    xtab_hbm,
    ytab_hbm,
    psi_ref,
    power_ref,
    xs_ref,
    ys_ref,
    wave_ref,
    ztab_ref,
    xtab_ref,
    ytab_ref,
    send_ref,
    land_ref,
    grid_ref,
    mid_ref,
    sems,
    send_sems,
    recv_sems,
):
    me = lax.axis_index("fft")
    loads = [
        pltpu.make_async_copy(source, target, sems.at[i])
        for i, (source, target) in enumerate(
            [(wave_hbm, wave_ref), (ztab_hbm, ztab_ref), (xtab_hbm, xtab_ref), (ytab_hbm, ytab_ref)]
        )
    ]
    for load in loads:
        load.start()
    barrier = pltpu.get_barrier_semaphore()
    greet(barrier, me)
    loads[0].wait()
    loads[1].wait()

    x, y = grid_xy(stick_ref)
    half = N // 2
    xc = jnp.where(x < half, x, x - N) + SHIFT
    yc = jnp.where(y < half, y, y - N) + SHIFT
    both = [jnp.concatenate([wave_ref[0, b], wave_ref[1, b]], axis=0) for b in range(2)]
    result = dot(ztab_ref[...], rhs3(jnp.concatenate(both, axis=1)))
    for b in range(2):
        send_ref[:, 8 * b : 8 * b + 8, :] = result[:, 128 * b : 128 * b + 128].reshape(
            N_FFT, 8, 128
        )
    send_ref[:, 6:7, :] = jnp.broadcast_to(xc[None], (N_FFT, 1, 128))
    send_ref[:, 7:8, :] = jnp.broadcast_to(yc[None], (N_FFT, 1, 128))

    pl.semaphore_wait(barrier, N_FFT - 1)

    def send(step, carry):
        exchange_copy(send_ref, land_ref, send_sems, recv_sems, me, step).start()
        return carry

    lax.fori_loop(1, N_FFT, send, 0)
    land_ref[me] = send_ref[me]

    grid_ref[...] = jnp.zeros_like(grid_ref)
    row_id = lax.broadcasted_iota(jnp.int32, (HALF, 128), 0).astype(F32)
    lane_id = lax.broadcasted_iota(jnp.int32, (256, 128), 0).astype(F32)

    def scatter(chunk, carry):
        lefts, rights = [], []
        for i in range(CHUNK):
            step = chunk * CHUNK + i

            @pl.when(step > 0)
            def _():
                landing(send_ref, land_ref, send_sems, recv_sems, me, step).wait_recv()

            tile = land_ref[shifted(me, step, -1)]
            x, y = tile[6:7], tile[7:8]
            x2 = jnp.floor(x * 0.5)
            here = row_id == x2
            spot = (lane_id == (x - 2.0 * x2) * 128.0 + y).astype(F32).astype(BF16)
            high = tile.astype(BF16).astype(F32)
            low = tile - high
            for piece in (high, low):
                picked = [
                    jnp.where(here, piece[8 * b + 3 * o + s : 8 * b + 3 * o + s + 1], 0.0)
                    for b, o, s in ROWS
                ]
                lefts.append(jnp.concatenate(picked, axis=0).astype(BF16))
                rights.append(spot)
        grid_ref[...] += dot_nt(jnp.concatenate(lefts, axis=1), jnp.concatenate(rights, axis=1))
        return carry

    lax.fori_loop(0, N_FFT // CHUNK, scatter, 0)
    xs_ref[...] = land_ref[:, 6, :]
    ys_ref[...] = land_ref[:, 7, :]

    columns = []
    for b in range(2):
        for s in range(ZP):
            rows = []
            for o in range(2):
                first = (b * 6 + o * 3 + s) * HALF
                for parity in range(2):
                    rows.append(
                        grid_ref[first : first + HALF, 128 * parity : 128 * parity + 128]
                    )
            columns.append(jnp.concatenate(rows, axis=0))
    loads[2].wait()
    mixed = dot(xtab_ref[...], rhs3(jnp.concatenate(columns, axis=1)))
    for g in range(4):
        for o in range(2):
            first = (o * 4 + g) * 40
            for bs in range(6):
                mid_ref[g, 40 * bs : 40 * bs + 40, 128 * o : 128 * o + 128] = mixed[
                    first : first + 40, 128 * bs : 128 * bs + 128
                ]
    lefts = [lhs3(mid_ref[g]) for g in range(4)]
    loads[3].wait()
    for j in range(5):
        total = None
        for at, (tile, g) in enumerate(PAIRS):
            if tile == j:
                high, low = ytab_ref[at, 0], ytab_ref[at, 1]
                term = dot(lefts[g], jnp.concatenate([high, low, high], axis=0))
                total = term if total is None else total + term
        for b in range(2):
            for s in range(ZP):
                bs = b * ZP + s
                for o in range(2):
                    first = s * 200 + j * 40
                    psi_ref[b * 2 + o, first : first + 40, :] = total[
                        40 * bs : 40 * bs + 40, 128 * o : 128 * o + 128
                    ]

    def power(b):
        re, im = psi_ref[2 * b], psi_ref[2 * b + 1]
        return re * re + im * im

    power_ref[:600] = occ_ref[0] * power(0) + occ_ref[1] * power(1)
    power_ref[600:] = jnp.zeros((4 * SLICE - 600, 128), F32)

    def sent(step, carry):
        exchange_copy(send_ref, land_ref, send_sems, recv_sems, me, step).wait_send()
        return carry

    lax.fori_loop(1, N_FFT, sent, 0)


def project(place_ref, atom_ref, psi_ref, proj_hbm, sums_ref, proj_ref, acc_ref, sems):
    proj_copy = pltpu.make_async_copy(proj_hbm, proj_ref, sems.at[0])
    proj_copy.start()
    acc_ref[...] = jnp.zeros_like(acc_ref)
    base = lax.axis_index("fft") * ATOM_DEV - ATOM_DEV // 2
    proj_copy.wait()

    def one(k, carry):
        row = block_row(place_ref[k])
        first = ((atom_ref[k] - base) & (ATOMS - 1)) * 4
        values = proj_ref[k]
        for c in range(4):
            acc_ref[first + c] += values * psi_ref[c, pl.ds(row, 1), :]
        return carry

    lax.fori_loop(0, NBLK, one, 0)
    ones = jnp.ones((256, 128), BF16)
    lane = lax.broadcasted_iota(jnp.int32, (64, 128), 1)
    sums = jnp.zeros((64, 128), F32)
    for chunk in range(8):
        high, low = split(acc_ref[16 * chunk : 16 * chunk + 16].reshape(1024, 128))
        total = dot(jnp.concatenate([high, low], axis=1), ones)
        for m in range(16):
            sums = jnp.where(lane == chunk * 16 + m, total[64 * m : 64 * m + 64], sums)
    sums_ref[...] = sums


def apply_local(
    place_ref,
    atom_ref,
    sums_ref,
    before_ref,
    after_ref,
    coupling_ref,
    psi_ref,
    potential_ref,
    proj_hbm,
    h_ref,
    weight_ref,
    pot_ref,
    proj_ref,
    sems,
):
    proj_copy = pltpu.make_async_copy(proj_hbm, proj_ref, sems.at[0])
    proj_copy.start()
    for q in range(200):
        row = (q % 5) * 40 + q // 5
        pot_ref[:, row, :] = potential_ref[:, 128 * q : 128 * q + 128]
    potential = pot_ref[...].reshape(600, 128)
    for c in range(4):
        h_ref[c] = potential * psi_ref[c]

    lane = lax.broadcasted_iota(jnp.int32, (64, 128), 1)
    beside = jnp.where(
        lane < 64, pltpu.roll(before_ref[...], 64, 1), pltpu.roll(after_ref[...], 64, 1)
    )
    combined = sums_ref[...] + beside
    weight = lax.dot_general(
        coupling_ref[...],
        combined,
        (((1,), (0,)), ((), ())),
        precision=lax.Precision.HIGHEST,
        preferred_element_type=F32,
    )
    for n in range(128):
        weight_ref[n] = jnp.broadcast_to(weight[:, n : n + 1], (64, 128))
    base = lax.axis_index("fft") * ATOM_DEV - ATOM_DEV // 2
    proj_copy.wait()

    def add(k, carry):
        row = block_row(place_ref[k])
        first = ((atom_ref[k] - base) & (ATOMS - 1)) * 4
        values = proj_ref[k]
        for c in range(4):
            h_ref[c, pl.ds(row, 1), :] += jnp.sum(
                values * weight_ref[first + c], axis=0, keepdims=True
            )
        return carry

    lax.fori_loop(0, NBLK, add, 0)


def slice_copy(source, target, send_sems, recv_sems, at, device):
    return pltpu.make_async_remote_copy(
        src_ref=source,
        dst_ref=target,
        send_sem=send_sems.at[at],
        recv_sem=recv_sems.at[at],
        device_id={"band": device},
        device_id_type=pl.DeviceIdType.MESH,
    )


def to_sticks(
    xs_ref,
    ys_ref,
    stick_ref,
    h_ref,
    power_ref,
    core_ref,
    wave_hbm,
    ztab_hbm,
    xtab_hbm,
    ytab_hbm,
    out_ref,
    dens_ref,
    field_ref,
    wave_ref,
    ztab_ref,
    xtab_ref,
    ytab_ref,
    send_ref,
    land_ref,
    plane_ref,
    left_ref,
    part_ref,
    full_ref,
    mine_ref,
    box_ref,
    core3_ref,
    sems,
    send_sems,
    recv_sems,
    band_send_sems,
    band_recv_sems,
):
    me = lax.axis_index("fft")
    group = lax.axis_index("band")
    loads = [
        pltpu.make_async_copy(source, target, sems.at[i])
        for i, (source, target) in enumerate(
            [(ytab_hbm, ytab_ref), (xtab_hbm, xtab_ref), (wave_hbm, wave_ref), (ztab_hbm, ztab_ref)]
        )
    ]
    for load in loads:
        load.start()
    barrier = pltpu.get_barrier_semaphore()
    for step in range(1, 4):
        pl.semaphore_signal(
            barrier,
            inc=1,
            device_id={"band": lax.rem(group + step, 4)},
            device_id_type=pl.DeviceIdType.MESH,
        )
    greet(barrier, me)

    lefts = []
    for j in range(5):
        rows = []
        for b in range(2):
            for s in range(ZP):
                first = s * 200 + j * 40
                rows.append(
                    jnp.concatenate(
                        [h_ref[b * 2 + o, first : first + 40, :] for o in range(2)], axis=1
                    )
                )
        lefts.append(lhs3(jnp.concatenate(rows, axis=0)))
    loads[0].wait()
    turned = []
    for g in range(4):
        total = None
        for at, (j, owner) in enumerate(PAIRS):
            if owner == g:
                high, low = ytab_ref[at, 0], ytab_ref[at, 1]
                term = dot(lefts[j], jnp.concatenate([high, low, high], axis=0))
                total = term if total is None else total + term
        turned.append(total)

    pl.semaphore_wait(barrier, N_FFT - 1 + 3)

    def rows_of(index):
        return pl.ds(pl.multiple_of(index * SLICE, 8), SLICE)

    def quarter(step):
        target = lax.rem(group + step, 4)
        return slice_copy(
            power_ref.at[rows_of(target)],
            part_ref.at[step - 1],
            band_send_sems,
            band_recv_sems,
            step - 1,
            target,
        )

    for step in range(1, 4):
        quarter(step).start()

    columns = []
    for bs in range(6):
        rows = []
        for o in range(2):
            for g in range(4):
                rows.append(turned[g][40 * bs : 40 * bs + 40, 128 * o : 128 * o + 128])
        columns.append(jnp.concatenate(rows, axis=0))
    loads[1].wait()
    spectrum = dot(xtab_ref[...], rhs3(jnp.concatenate(columns, axis=1)))
    for at, (b, o, s) in enumerate(ROWS):
        bs = b * ZP + s
        plane_ref[at * BOX : at * BOX + BOX, :] = spectrum[
            o * BOX : o * BOX + BOX, 128 * bs : 128 * bs + 128
        ]
    high, low = split(plane_ref[...])
    left_ref[:, :128] = high
    left_ref[:, 128:] = low

    row_id = lax.broadcasted_iota(jnp.int32, (128, 256), 0).astype(F32)
    zeros = jnp.zeros((2, 256), F32)

    def gather(pair, carry):
        steps = (2 * pair, 2 * pair + 1)
        targets = [shifted(me, step, 1) for step in steps]
        x = jnp.concatenate([xs_ref[pl.ds(t, 1), :] for t in targets], axis=1)
        y = jnp.concatenate([ys_ref[pl.ds(t, 1), :] for t in targets], axis=1)
        spot = (row_id == y).astype(F32).astype(BF16)
        values = dot(left_ref[...], jnp.concatenate([spot, spot], axis=0))
        here = row_id[:BOX] == x
        rows = []
        for at in range(12):
            masked = jnp.where(here, values[at * BOX : at * BOX + BOX], 0.0)
            rows.append(jnp.sum(masked, axis=0, keepdims=True))
            if at % 6 == 5:
                rows.append(zeros)
        result = jnp.concatenate(rows, axis=0)
        send_ref[targets[0]] = result[:, :128]
        send_ref[targets[1]] = result[:, 128:]

        @pl.when(pair > 0)
        def _():
            exchange_copy(send_ref, land_ref, send_sems, recv_sems, me, steps[0]).start()

        exchange_copy(send_ref, land_ref, send_sems, recv_sems, me, steps[1]).start()
        return carry

    lax.fori_loop(0, N_FFT // 4, gather, 0)

    for step in range(1, 4):
        quarter(step).wait()
    mine = power_ref[rows_of(group)]
    mine_ref[...] = mine + part_ref[0] + part_ref[1] + part_ref[2]
    full_ref[rows_of(group)] = mine_ref[...]

    def whole(step):
        return slice_copy(
            mine_ref,
            full_ref.at[rows_of(group)],
            band_send_sems,
            band_recv_sems,
            2 + step,
            lax.rem(group + step, 4),
        )

    for step in range(1, 4):
        whole(step).start()

    lax.fori_loop(N_FFT // 4, N_FFT // 2, gather, 0)
    land_ref[me] = send_ref[me]

    for q in range(200):
        row = (q % 5) * 40 + q // 5
        core3_ref[:, row, :] = core_ref[:, 128 * q : 128 * q + 128]
    for step in range(1, 4):
        source = lax.rem(group + 4 - step, 4)
        slice_copy(
            mine_ref,
            full_ref.at[rows_of(source)],
            band_send_sems,
            band_recv_sems,
            2 + step,
            source,
        ).wait_recv()
    for step in range(1, 4):
        whole(step).wait_send()
    density = full_ref[:600].reshape(ZP, 200, 128)
    box_ref[...] = density
    for q in range(200):
        row = (q % 5) * 40 + q // 5
        dens_ref[:, 128 * q : 128 * q + 128] = box_ref[:, row, :]
    slot = lax.broadcasted_iota(jnp.int32, (ZP, 200, 128), 0)
    field = -lda_factor * jnp.exp(jnp.log(density + core3_ref[...]) * (1.0 / 3.0))
    core3_ref[...] = jnp.where(slot * N_FFT + me < N, field, 0.0)
    for q in range(200):
        row = (q % 5) * 40 + q // 5
        field_ref[:, 128 * q : 128 * q + 128] = core3_ref[:, row, :]

    loads[2].wait()
    x, y = grid_xy(stick_ref)
    half = N // 2
    x = jnp.where(x < half, x, x - N) / N
    y = jnp.where(y < half, y, y - N) / N
    g = lax.broadcasted_iota(jnp.int32, (N, 128), 0)
    z = jnp.where(g < half, g, g - N).astype(F32) / N
    kinetic = 2.0 * (x * x + y * y) + 2.0 * (z * z)
    loads[3].wait()

    def arrive(step, carry):
        landing(send_ref, land_ref, send_sems, recv_sems, me, step).wait_recv()
        return carry

    lax.fori_loop(1, N_FFT, arrive, 0)
    both = [land_ref[:, 8 * b : 8 * b + 8, :].reshape(N_FFT * 8, 128) for b in range(2)]
    result = dot(ztab_ref[...], rhs3(jnp.concatenate(both, axis=1)))
    for o in range(2):
        for b in range(2):
            spectrum = result[N * o : N * o + N, 128 * b : 128 * b + 128]
            out_ref[o, b] = spectrum + kinetic * wave_ref[o, b]

    def sent(step, carry):
        exchange_copy(send_ref, land_ref, send_sems, recv_sems, me, step).wait_send()
        return carry

    lax.fori_loop(1, N_FFT, sent, 0)


VMEM = pltpu.VMEM
DMA = pltpu.SemaphoreType.DMA
SMEM_SPEC = pl.BlockSpec(memory_space=pltpu.SMEM)
VMEM_SPEC = pl.BlockSpec(memory_space=pltpu.VMEM)
ANY_SPEC = pl.BlockSpec(memory_space=pl.ANY)
LIMIT = 56 * 1024 * 1024


def call(body, in_specs, outs, scratch=(), flops=0, size=0, remote=None):
    options = {} if remote is None else dict(collective_id=remote, has_side_effects=True)
    return pl.pallas_call(
        body,
        out_shape=outs,
        in_specs=in_specs,
        out_specs=jax.tree.map(lambda _: VMEM_SPEC, outs),
        scratch_shapes=list(scratch),
        compiler_params=pltpu.CompilerParams(vmem_limit_bytes=LIMIT, **options),
        cost_estimate=pl.CostEstimate(flops=flops, bytes_accessed=size, transcendentals=0),
    )


def shape(*dims):
    return jax.ShapeDtypeStruct(dims, F32)


def make_calls():
    wave = VMEM((2, 2, N, 128), F32)
    ytab = VMEM((8, 2, 256, 256), BF16)
    tiles = VMEM((N_FFT, 16, 128), F32)
    planes = call(
        to_planes,
        [SMEM_SPEC, VMEM_SPEC] + [ANY_SPEC] * 4,
        (shape(4, 600, 128), shape(4 * SLICE, 128), shape(N_FFT, 128), shape(N_FFT, 128)),
        (
            wave,
            VMEM((8 * N_FFT, 6 * N), BF16),
            VMEM((2 * N, 12 * HALF), BF16),
            ytab,
            tiles,
            tiles,
            VMEM((12 * HALF, 256), F32),
            VMEM((4, 240, 256), F32),
            DMA((4,)),
            DMA((N_FFT,)),
            DMA((N_FFT,)),
        ),
        10_000_000_000,
        8_000_000,
        0,
    )
    projected = call(
        project,
        [SMEM_SPEC] * 2 + [VMEM_SPEC, ANY_SPEC],
        shape(64, 128),
        (VMEM((NBLK, 64, 128), F32), VMEM((128, 64, 128), F32), DMA((1,))),
        1_000_000_000,
        8_000_000,
    )
    applied = call(
        apply_local,
        [SMEM_SPEC] * 2 + [VMEM_SPEC] * 6 + [ANY_SPEC],
        shape(4, 600, 128),
        (
            VMEM((128, 64, 128), F32),
            VMEM((ZP, 200, 128), F32),
            VMEM((NBLK, 64, 128), F32),
            DMA((1,)),
        ),
        1_000_000_000,
        8_000_000,
    )
    sticks = call(
        to_sticks,
        [VMEM_SPEC] * 6 + [ANY_SPEC] * 4,
        (shape(2, 2, N, 128), shape(ZP, N * N), shape(ZP, N * N)),
        (
            wave,
            VMEM((2 * N, 24 * N_FFT), BF16),
            VMEM((2 * BOX, 6 * N), BF16),
            ytab,
            tiles,
            tiles,
            VMEM((12 * BOX, 128), F32),
            VMEM((12 * BOX, 256), BF16),
            VMEM((3, SLICE, 128), F32),
            VMEM((4 * SLICE, 128), F32),
            VMEM((SLICE, 128), F32),
            VMEM((ZP, 200, 128), F32),
            VMEM((ZP, 200, 128), F32),
            DMA((4,)),
            DMA((N_FFT,)),
            DMA((N_FFT,)),
            DMA((6,)),
            DMA((6,)),
        ),
        10_000_000_000,
        8_000_000,
        1,
    )
    return planes, projected, applied, sticks


def local(
    tables,
    wave_coef,
    stick_map,
    local_potential,
    core_density,
    occupations,
    block_place,
    block_atom,
    projectors,
    coupling,
):
    planes, projected, applied, sticks = make_calls()
    stick_row = stick_map.reshape(1, 128)
    psi, power, xs, ys = planes(
        occupations,
        stick_row,
        wave_coef,
        tables["z_ahead"],
        tables["x_ahead"],
        tables["y_ahead"],
    )
    sums = projected(block_place, block_atom, psi, projectors)
    up = [(i, (i + 1) % N_FFT) for i in range(N_FFT)]
    down = [(j, i) for i, j in up]
    before = lax.ppermute(sums, "fft", up)
    after = lax.ppermute(sums, "fft", down)
    h = applied(
        block_place, block_atom, sums, before, after, coupling, psi, local_potential, projectors
    )
    return sticks(
        xs,
        ys,
        stick_row,
        h,
        power,
        core_density,
        wave_coef,
        tables["z_back"],
        tables["x_back"],
        tables["y_back"],
    )


def solution(mesh):
    tables = {name: jnp.asarray(value) for name, value in make_tables().items()}

    def run(*args):
        return local(tables, *args)

    return jax.shard_map(
        run,
        mesh=mesh,
        in_specs=(
            P(None, "band", None, "fft"),
            P("fft"),
            P("fft", None),
            P("fft", None),
            P("band"),
            P("fft"),
            P("fft"),
            P("fft", None, None),
            P(),
        ),
        out_specs=(P(None, "band", None, "fft"), P("fft", None), P("fft", None)),
        check_vma=False,
    )
```

```python
import math

import jax
import jax.numpy as jnp
import numpy as np
from jax import lax
from jax.experimental import pallas as pl
from jax.experimental.pallas import tpu as pltpu
from jax.sharding import PartitionSpec as P

N = 160
ZP = 3
N_FFT = 64
NBLK = 96
ATOM_DEV = 16
ATOMS = 1024
BANDS_AXIS = 4
SLICE = 152
SHIFT = 52
BOX = 104
HALF = 56
F32 = jnp.float32
BF16 = jnp.bfloat16

lda_factor = (3.0 / math.pi) ** (1.0 / 3.0)


def parts(table):
    high = table.astype(np.float32).astype(jnp.bfloat16)
    low = (table - high.astype(np.float64)).astype(np.float32).astype(jnp.bfloat16)
    return high, low


def real_form(cosine, sine):
    return np.block([[cosine, -sine], [sine, cosine]])


def z_tables():
    slot, place = np.meshgrid(np.arange(8), np.arange(N_FFT), indexing="ij")
    out = np.zeros((N_FFT, 8, 2, N))
    g = np.arange(N)
    for f in range(N_FFT):
        for s in range(ZP):
            z = s * N_FFT + f
            if z < N:
                phase = 2 * np.pi / N * ((z * g) % N)
                c, d = np.cos(phase) / math.sqrt(N), np.sin(phase) / math.sqrt(N)
                out[f, s, 0], out[f, s, 1] = c, -d
                out[f, 3 + s, 0], out[f, 3 + s, 1] = d, c
    forward = out.reshape(N_FFT * 8, 2 * N)
    return forward, forward.T


def x_tables():
    rows = np.array([4 * k + g for g in range(4) for k in range(40)])
    compact = np.array([2 * h + p for p in range(2) for h in range(HALF)])
    phase = 2 * np.pi / N * ((rows[:, None] * (compact[None, :] - SHIFT)) % N)
    keep = (compact < BOX)[None, :] / math.sqrt(N)
    ahead = real_form(np.cos(phase) * keep, np.sin(phase) * keep)
    phase = phase.T
    keep = keep.T
    back = real_form(np.cos(phase) * keep, -np.sin(phase) * keep)
    return ahead, back


PAIRS = tuple((j, g) for g in range(4) for j in (g, g + 1))


def y_tables():
    compact = np.arange(128)
    out = []
    for j, g in PAIRS:
        flat = 128 * j + np.arange(128)
        keep = ((flat // N == g)[None, :] & (compact < BOX)[:, None]) / math.sqrt(N)
        phase = 2 * np.pi / N * (((compact[:, None] - SHIFT) * (flat % N)[None, :]) % N)
        c, d = np.cos(phase) * keep, np.sin(phase) * keep
        out.append(np.block([[c, d], [-d, c]]))
    return np.stack(out)


def stack3(table, axis):
    high, low = parts(table)
    return np.concatenate([high, low, high], axis=axis)


def make_tables():
    z_ahead, z_back = z_tables()
    x_ahead, x_back = x_tables()
    y_ahead = y_tables()
    y_back = np.swapaxes(y_ahead, 1, 2)
    return dict(
        z_ahead=stack3(z_ahead, 1),
        z_back=stack3(z_back, 1),
        x_ahead=stack3(x_ahead, 1),
        x_back=stack3(x_back, 1),
        y_ahead=np.stack(parts(y_ahead), axis=1),
        y_back=np.stack(parts(y_back), axis=1),
    )


def split(value):
    high = value.astype(BF16)
    return high, (value - high.astype(F32)).astype(BF16)


def dot(left, right):
    return lax.dot_general(left, right, (((1,), (0,)), ((), ())), preferred_element_type=F32)


def dot_nt(left, right):
    return lax.dot_general(left, right, (((1,), (1,)), ((), ())), preferred_element_type=F32)


def lhs3(value):
    high, low = split(value)
    return jnp.concatenate([high, high, low], axis=1)


def rhs3(value):
    high, low = split(value)
    return jnp.concatenate([high, high, low], axis=0)


def grid_xy(stick_ref):
    column = stick_ref[...].astype(F32)
    x = jnp.floor((column + 0.5) * (1.0 / N))
    y = column - N * x
    return x, y


def block_row(place):
    slot = (place >= 200).astype(jnp.int32) + (place >= 400).astype(jnp.int32)
    inside = place - 200 * slot
    fifth = (inside * 6554) >> 15
    return slot * 200 + (inside - 5 * fifth) * 40 + fifth


ROWS = [(b, o, s) for b in range(2) for o in range(2) for s in range(ZP)]
CHUNK = 4
PART = 12 * HALF


def ahead_of(me, step):
    return lax.rem(me + step, N_FFT)


def behind(me, step):
    return lax.rem(me + N_FFT - step, N_FFT)


def fft_copy(source, target, send_sem, recv_sem, device):
    return pltpu.make_async_remote_copy(
        src_ref=source,
        dst_ref=target,
        send_sem=send_sem,
        recv_sem=recv_sem,
        device_id={"fft": device},
        device_id_type=pl.DeviceIdType.MESH,
    )


def band_copy(source, target, send_sem, recv_sem, device):
    return pltpu.make_async_remote_copy(
        src_ref=source,
        dst_ref=target,
        send_sem=send_sem,
        recv_sem=recv_sem,
        device_id={"band": device},
        device_id_type=pl.DeviceIdType.MESH,
    )


def put(send_ref, land_ref, send_sems, recv_sems, me, step):
    target = ahead_of(me, step)
    return fft_copy(
        send_ref.at[target], land_ref.at[me], send_sems.at[step], recv_sems.at[step], target
    )


def landing(send_ref, land_ref, send_sems, recv_sems, me, step):
    source = behind(me, step)
    return fft_copy(
        send_ref.at[source], land_ref.at[source], send_sems.at[step], recv_sems.at[step], source
    )


def whole(
    occ_ref,
    place_ref,
    atom_ref,
    place_row_ref,
    atom_row_ref,
    stick_ref,
    coupling_ref,
    potential_ref,
    wave_hbm,
    ztab_hbm,
    xtab_hbm,
    ytab_hbm,
    proj_hbm,
    xback_hbm,
    yback_hbm,
    land_ref,
    full_ref,
    wave_ref,
    ztab_ref,
    xtab_ref,
    ytab_ref,
    proj_ref,
    xback_ref,
    yback_ref,
    send_ref,
    first_ref,
    last_ref,
    grid_ref,
    mid_ref,
    psi_ref,
    power_ref,
    piece_ref,
    sums_ref,
    before_ref,
    after_ref,
    weight_ref,
    pot_ref,
    add_ref,
    h_ref,
    left_ref,
    part_ref,
    mine_ref,
    total_ref,
    sems,
    send_sems,
    recv_sems,
    send2_sems,
    recv2_sems,
    halo_send_sems,
    halo_recv_sems,
    band_send_sems,
    band_recv_sems,
):
    me = lax.axis_index("fft")
    group = lax.axis_index("band")
    barrier = pltpu.get_barrier_semaphore()
    loads = [
        pltpu.make_async_copy(source, target, sems.at[i])
        for i, (source, target) in enumerate(
            [
                (wave_hbm, wave_ref),
                (ztab_hbm, ztab_ref),
                (xtab_hbm, xtab_ref),
                (ytab_hbm, ytab_ref),
                (proj_hbm, proj_ref),
                (xback_hbm, xback_ref),
                (yback_hbm, yback_ref),
            ]
        )
    ]
    for load in loads:
        load.start()

    def greet(step, carry):
        pl.semaphore_signal(
            barrier,
            inc=1,
            device_id={"fft": ahead_of(me, step)},
            device_id_type=pl.DeviceIdType.MESH,
        )
        return carry

    lax.fori_loop(1, N_FFT, greet, 0, unroll=3)
    for step in range(1, 4):
        pl.semaphore_signal(
            barrier,
            inc=1,
            device_id={"band": lax.rem(group + step, 4)},
            device_id_type=pl.DeviceIdType.MESH,
        )

    grid_ref[...] = jnp.zeros_like(grid_ref)
    x, y = grid_xy(stick_ref)
    half = N // 2
    xc = jnp.where(x < half, x, x - N) + SHIFT
    yc = jnp.where(y < half, y, y - N) + SHIFT
    loads[0].wait()
    loads[1].wait()
    both = [jnp.concatenate([wave_ref[0, b], wave_ref[1, b]], axis=0) for b in range(2)]
    result = dot(ztab_ref[...], rhs3(jnp.concatenate(both, axis=1)))
    for b in range(2):
        send_ref[:, 8 * b : 8 * b + 8, :] = result[:, 128 * b : 128 * b + 128].reshape(
            N_FFT, 8, 128
        )
    send_ref[:, 6:7, :] = jnp.broadcast_to(xc[None], (N_FFT, 1, 128))
    send_ref[:, 7:8, :] = jnp.broadcast_to(yc[None], (N_FFT, 1, 128))

    pl.semaphore_wait(barrier, N_FFT - 1 + 3)

    def send(step, carry):
        put(send_ref, first_ref, send_sems, recv_sems, me, step).start()
        return carry

    lax.fori_loop(1, N_FFT, send, 0, unroll=3)
    first_ref[me] = send_ref[me]

    row_id = lax.broadcasted_iota(jnp.int32, (HALF, 128), 0).astype(F32)
    lane_id = lax.broadcasted_iota(jnp.int32, (256, 128), 0).astype(F32)

    def scatter(chunk, carry):
        lefts, rights = [], []
        for i in range(CHUNK):
            step = chunk * CHUNK + i

            @pl.when(step > 0)
            def _():
                landing(send_ref, first_ref, send_sems, recv_sems, me, step).wait_recv()

            tile = first_ref[behind(me, step)]
            x, y = tile[6:7], tile[7:8]
            x2 = jnp.floor(x * 0.5)
            here = row_id == x2
            rights.append((lane_id == (x - 2.0 * x2) * 128.0 + y).astype(F32).astype(BF16))
            high = tile.astype(BF16).astype(F32)
            picked = [
                jnp.where(here, piece[8 * b + 3 * o + s : 8 * b + 3 * o + s + 1], 0.0)
                for piece in (high, tile - high)
                for b, o, s in ROWS
            ]
            lefts.append(jnp.concatenate(picked, axis=0).astype(BF16))
        grid_ref[...] += dot_nt(jnp.concatenate(lefts, axis=1), jnp.concatenate(rights, axis=1))
        return carry

    lax.fori_loop(0, N_FFT // CHUNK, scatter, 0)

    columns = []
    for b in range(2):
        for s in range(ZP):
            rows = []
            for o in range(2):
                first = (b * 6 + o * 3 + s) * HALF
                for parity in range(2):
                    lanes = slice(128 * parity, 128 * parity + 128)
                    rows.append(
                        grid_ref[first : first + HALF, lanes]
                        + grid_ref[PART + first : PART + first + HALF, lanes]
                    )
            columns.append(jnp.concatenate(rows, axis=0))
    loads[2].wait()
    mixed = dot(xtab_ref[...], rhs3(jnp.concatenate(columns, axis=1)))
    for g in range(4):
        for o in range(2):
            first = (o * 4 + g) * 40
            for bs in range(6):
                mid_ref[g, 40 * bs : 40 * bs + 40, 128 * o : 128 * o + 128] = mixed[
                    first : first + 40, 128 * bs : 128 * bs + 128
                ]
    lefts = [lhs3(mid_ref[g]) for g in range(4)]
    loads[3].wait()
    for j in range(5):
        total = None
        for at, (tile, g) in enumerate(PAIRS):
            if tile == j:
                high, low = ytab_ref[at, 0], ytab_ref[at, 1]
                term = dot(lefts[g], jnp.concatenate([high, low, high], axis=0))
                total = term if total is None else total + term
        for b in range(2):
            for s in range(ZP):
                bs = b * ZP + s
                for o in range(2):
                    first = s * 200 + j * 40
                    psi_ref[b * 2 + o, first : first + 40, :] = total[
                        40 * bs : 40 * bs + 40, 128 * o : 128 * o + 128
                    ]

    def power(b):
        re, im = psi_ref[2 * b], psi_ref[2 * b + 1]
        return re * re + im * im

    power_ref[:600] = occ_ref[0] * power(0) + occ_ref[1] * power(1)
    power_ref[600:] = jnp.zeros((4 * SLICE - 600, 128), F32)

    def rows_of(index):
        return pl.ds(pl.multiple_of(index * SLICE, 8), SLICE)

    def quarter(step):
        target = lax.rem(group + step, 4)
        return band_copy(
            power_ref.at[rows_of(target)],
            part_ref.at[step - 1],
            band_send_sems.at[step - 1],
            band_recv_sems.at[step - 1],
            target,
        )

    for step in range(1, 4):
        quarter(step).start()

    def fetch(k, carry):
        row = block_row(place_ref[k])
        for c in range(4):
            piece_ref[pl.ds(4 * k + c, 1), :] = psi_ref[c, pl.ds(row, 1), :]
        return carry

    lax.fori_loop(0, NBLK, fetch, 0, unroll=4)
    loads[4].wait()
    lane = lax.broadcasted_iota(jnp.int32, (64, 128), 1)
    picks = []
    for part in range(3):
        piece_high, piece_low = split(piece_ref[128 * part : 128 * part + 128])
        piece_both = jnp.concatenate([piece_high, piece_high], axis=1)
        found = jnp.zeros((64, 128), F32)
        for chunk in range(2):
            first = part * 32 + chunk * 16
            high, low = split(proj_ref[first : first + 16].reshape(1024, 128))
            values = dot_nt(jnp.concatenate([high, low], axis=1), piece_both)
            values = values + dot_nt(high, piece_low)
            for m in range(16):
                own = lax.div(lane, 4) == chunk * 16 + m
                found = jnp.where(own, values[64 * m : 64 * m + 64], found)
        picks.append(found)
    found = jnp.concatenate(picks, axis=1)
    base = me * ATOM_DEV - ATOM_DEV // 2
    near = lax.rem(atom_row_ref[...] - base + 2 * ATOMS, ATOMS).astype(F32)
    spread = lax.div(lax.broadcasted_iota(jnp.int32, (NBLK, 4 * NBLK), 1), 4)
    spread = spread == lax.broadcasted_iota(jnp.int32, (NBLK, 4 * NBLK), 0)
    near = dot(
        jnp.broadcast_to(near, (16, NBLK)).astype(BF16), spread.astype(F32).astype(BF16)
    )[0:1]
    column = lax.broadcasted_iota(jnp.int32, (128, 4 * NBLK), 0)
    owner = lax.rem(lax.broadcasted_iota(jnp.int32, (128, 4 * NBLK), 1), 4).astype(F32) + 4.0 * near
    member = (owner == column.astype(F32)).astype(F32).astype(BF16)
    high, low = split(found)
    sums_ref[...] = dot_nt(
        jnp.concatenate([high, low], axis=1), jnp.concatenate([member, member], axis=1)
    )
    after_me, before_me = ahead_of(me, 1), behind(me, 1)
    to_after = fft_copy(
        sums_ref, before_ref, halo_send_sems.at[0], halo_recv_sems.at[0], after_me
    )
    to_before = fft_copy(
        sums_ref, after_ref, halo_send_sems.at[1], halo_recv_sems.at[1], before_me
    )
    to_after.start()
    to_before.start()

    for q in range(200):
        row = (q % 5) * 40 + q // 5
        pot_ref[:, row, :] = potential_ref[:, 128 * q : 128 * q + 128]

    for step in range(1, 4):
        quarter(step).wait()
    mine_ref[...] = power_ref[rows_of(group)] + part_ref[0] + part_ref[1] + part_ref[2]
    total_ref[rows_of(group)] = mine_ref[...]

    def share(step):
        return band_copy(
            mine_ref,
            total_ref.at[rows_of(group)],
            band_send_sems.at[2 + step],
            band_recv_sems.at[2 + step],
            lax.rem(group + step, 4),
        )

    for step in range(1, 4):
        share(step).start()

    to_after.wait()
    to_before.wait()
    beside = jnp.where(
        lane < 64, pltpu.roll(before_ref[...], 64, 1), pltpu.roll(after_ref[...], 64, 1)
    )
    weight = lax.dot_general(
        coupling_ref[...],
        sums_ref[...] + beside,
        (((1,), (0,)), ((), ())),
        precision=lax.Precision.HIGHEST,
        preferred_element_type=F32,
    )
    for n in range(128):
        weight_ref[n] = jnp.broadcast_to(weight[:, n : n + 1], (64, 128))

    def added(k, carry):
        first = ((atom_ref[k] - base) & (2 * ATOM_DEV - 1)) * 4
        values = proj_ref[k]
        for c in range(4):
            add_ref[c, pl.ds(k, 1), :] = jnp.sum(
                values * weight_ref[first + c], axis=0, keepdims=True
            )
        return carry

    lax.fori_loop(0, NBLK, added, 0, unroll=2)
    place = place_row_ref[...]
    slot = (place >= 200).astype(jnp.int32) + (place >= 400).astype(jnp.int32)
    inside = place - 200 * slot
    fifth = (inside * 6554) >> 15
    place = slot * 200 + (inside - 5 * fifth) * 40 + fifth
    block_id = lax.broadcasted_iota(jnp.int32, (600, NBLK), 0)
    spot = (block_id == place).astype(F32).astype(BF16)
    potential = pot_ref[...].reshape(600, 128)
    for c in range(4):
        high, low = split(add_ref[c])
        h_ref[c] = potential * psi_ref[c] + (dot(spot, high) + dot(spot, low))

    lefts = []
    for j in range(5):
        rows = []
        for b in range(2):
            for s in range(ZP):
                first = s * 200 + j * 40
                rows.append(
                    jnp.concatenate(
                        [h_ref[b * 2 + o, first : first + 40, :] for o in range(2)], axis=1
                    )
                )
        lefts.append(lhs3(jnp.concatenate(rows, axis=0)))
    loads[6].wait()
    turned = []
    for g in range(4):
        total = None
        for at, (j, owner) in enumerate(PAIRS):
            if owner == g:
                high, low = yback_ref[at, 0], yback_ref[at, 1]
                term = dot(lefts[j], jnp.concatenate([high, low, high], axis=0))
                total = term if total is None else total + term
        turned.append(total)
    columns = []
    for bs in range(6):
        rows = []
        for o in range(2):
            for g in range(4):
                rows.append(turned[g][40 * bs : 40 * bs + 40, 128 * o : 128 * o + 128])
        columns.append(jnp.concatenate(rows, axis=0))
    loads[5].wait()
    spectrum = dot(xback_ref[...], rhs3(jnp.concatenate(columns, axis=1)))
    for at, (b, o, s) in enumerate(ROWS):
        bs = b * ZP + s
        for parity in range(2):
            first = (o * 2 + parity) * HALF
            grid_ref[at * HALF : at * HALF + HALF, 128 * parity : 128 * parity + 128] = spectrum[
                first : first + HALF, 128 * bs : 128 * bs + 128
            ]
    high, low = split(grid_ref[:PART])
    left_ref[:PART] = high
    left_ref[PART:] = low

    id256 = lax.broadcasted_iota(jnp.int32, (256, 256), 0).astype(F32)
    zeros = jnp.zeros((2, 256), F32)

    def gather(pair, carry):
        steps = (2 * pair, 2 * pair + 1)
        targets = [ahead_of(me, step) for step in steps]
        tiles = [first_ref[target, 0:8, :] for target in targets]
        x = jnp.concatenate([tile[6:7] for tile in tiles], axis=1)
        y = jnp.concatenate([tile[7:8] for tile in tiles], axis=1)
        x2 = jnp.floor(x * 0.5)
        here = id256[:HALF] == x2
        spot = (id256 == (x - 2.0 * x2) * 128.0 + y).astype(F32).astype(BF16)
        values = dot(left_ref[...], spot)
        rows = []
        for at in range(12):
            first = at * HALF
            one = values[first : first + HALF] + values[PART + first : PART + first + HALF]
            rows.append(jnp.sum(jnp.where(here, one, 0.0), axis=0, keepdims=True))
            if at % 6 == 5:
                rows.append(zeros)
        result = jnp.concatenate(rows, axis=0)
        for i in range(2):
            send2_ref[targets[i]] = result[:, 128 * i : 128 * i + 128]

        @pl.when(pair > 0)
        def _():
            put(send2_ref, last_ref, send2_sems, recv2_sems, me, steps[0]).start()

        put(send2_ref, last_ref, send2_sems, recv2_sems, me, steps[1]).start()
        return carry

    def sent(step, carry):
        put(send_ref, first_ref, send_sems, recv_sems, me, step).wait_send()
        return carry

    lax.fori_loop(1, N_FFT, sent, 0, unroll=3)
    send2_ref = send_ref
    lax.fori_loop(0, N_FFT // 2, gather, 0)
    last_ref[me] = send2_ref[me]

    for step in range(1, 4):
        source = lax.rem(group + 4 - step, 4)
        band_copy(
            mine_ref,
            total_ref.at[rows_of(source)],
            band_send_sems.at[2 + step],
            band_recv_sems.at[2 + step],
            source,
        ).wait_recv()
    for step in range(1, 4):
        share(step).wait_send()
    full_ref[...] = total_ref[...]

    def arrive(step, carry):
        landing(send2_ref, last_ref, send2_sems, recv2_sems, me, step).wait_recv()
        return carry

    lax.fori_loop(1, N_FFT, arrive, 0, unroll=3)
    land_ref[...] = last_ref[...]

    def sent2(step, carry):
        put(send2_ref, last_ref, send2_sems, recv2_sems, me, step).wait_send()
        return carry

    lax.fori_loop(1, N_FFT, sent2, 0, unroll=3)


def finish(
    stick_ref,
    land_ref,
    full_ref,
    core_ref,
    wave_ref,
    ztab_ref,
    out_ref,
    dens_ref,
    field_ref,
    box_ref,
    core3_ref,
):
    me = lax.axis_index("fft")
    for q in range(200):
        row = (q % 5) * 40 + q // 5
        core3_ref[:, row, :] = core_ref[:, 128 * q : 128 * q + 128]
    density = full_ref[:600].reshape(ZP, 200, 128)
    box_ref[...] = density
    for q in range(200):
        row = (q % 5) * 40 + q // 5
        dens_ref[:, 128 * q : 128 * q + 128] = box_ref[:, row, :]
    slot = lax.broadcasted_iota(jnp.int32, (ZP, 200, 128), 0)
    field = -lda_factor * jnp.exp(jnp.log(density + core3_ref[...]) * (1.0 / 3.0))
    core3_ref[...] = jnp.where(slot * N_FFT + me < N, field, 0.0)
    for q in range(200):
        row = (q % 5) * 40 + q // 5
        field_ref[:, 128 * q : 128 * q + 128] = core3_ref[:, row, :]
    x, y = grid_xy(stick_ref)
    half = N // 2
    x = jnp.where(x < half, x, x - N) / N
    y = jnp.where(y < half, y, y - N) / N
    g = lax.broadcasted_iota(jnp.int32, (N, 128), 0)
    z = jnp.where(g < half, g, g - N).astype(F32) / N
    kinetic = 2.0 * (x * x + y * y) + 2.0 * (z * z)
    both = [land_ref[:, 8 * b : 8 * b + 8, :].reshape(N_FFT * 8, 128) for b in range(2)]
    result = dot(ztab_ref[...], rhs3(jnp.concatenate(both, axis=1)))
    for o in range(2):
        for b in range(2):
            spectrum = result[N * o : N * o + N, 128 * b : 128 * b + 128]
            out_ref[o, b] = spectrum + kinetic * wave_ref[o, b]


VMEM = pltpu.VMEM
DMA = pltpu.SemaphoreType.DMA
SMEM_SPEC = pl.BlockSpec(memory_space=pltpu.SMEM)
VMEM_SPEC = pl.BlockSpec(memory_space=pltpu.VMEM)
ANY_SPEC = pl.BlockSpec(memory_space=pl.ANY)
LIMIT = 56 * 1024 * 1024


def call(body, in_specs, outs, scratch=(), flops=0, size=0, remote=None):
    options = {} if remote is None else dict(collective_id=remote, has_side_effects=True)
    return pl.pallas_call(
        body,
        out_shape=outs,
        in_specs=in_specs,
        out_specs=jax.tree.map(lambda _: VMEM_SPEC, outs),
        scratch_shapes=list(scratch),
        compiler_params=pltpu.CompilerParams(vmem_limit_bytes=LIMIT, **options),
        cost_estimate=pl.CostEstimate(flops=flops, bytes_accessed=size, transcendentals=0),
    )


def shape(*dims):
    return jax.ShapeDtypeStruct(dims, F32)


def make_calls():
    ytab = VMEM((8, 2, 256, 256), BF16)
    tiles = VMEM((N_FFT, 16, 128), F32)
    block = VMEM((64, 128), F32)
    big = call(
        whole,
        [SMEM_SPEC] * 3 + [VMEM_SPEC] * 5 + [ANY_SPEC] * 7,
        (shape(N_FFT, 16, 128), shape(4 * SLICE, 128)),
        (
            VMEM((2, 2, N, 128), F32),
            VMEM((8 * N_FFT, 6 * N), BF16),
            VMEM((2 * N, 12 * HALF), BF16),
            ytab,
            VMEM((NBLK, 64, 128), F32),
            VMEM((4 * HALF, 6 * N), BF16),
            ytab,
            tiles,
            tiles,
            tiles,
            VMEM((2 * PART, 256), F32),
            VMEM((4, 240, 256), F32),
            VMEM((4, 600, 128), F32),
            VMEM((4 * SLICE, 128), F32),
            VMEM((4 * NBLK, 128), F32),
            block,
            block,
            block,
            VMEM((128, 64, 128), F32),
            VMEM((ZP, 200, 128), F32),
            VMEM((4, NBLK, 128), F32),
            VMEM((4, 600, 128), F32),
            VMEM((2 * PART, 256), BF16),
            VMEM((3, SLICE, 128), F32),
            VMEM((SLICE, 128), F32),
            VMEM((4 * SLICE, 128), F32),
            DMA((7,)),
            DMA((N_FFT,)),
            DMA((N_FFT,)),
            DMA((N_FFT,)),
            DMA((N_FFT,)),
            DMA((2,)),
            DMA((2,)),
            DMA((6,)),
            DMA((6,)),
        ),
        20_000_000_000,
        16_000_000,
        0,
    )
    last = call(
        finish,
        [VMEM_SPEC] * 6,
        (shape(2, 2, N, 128), shape(ZP, N * N), shape(ZP, N * N)),
        (VMEM((ZP, 200, 128), F32), VMEM((ZP, 200, 128), F32)),
        500_000_000,
        4_000_000,
    )
    return big, last


def local(
    tables,
    wave_coef,
    stick_map,
    local_potential,
    core_density,
    occupations,
    block_place,
    block_atom,
    projectors,
    coupling,
):
    big, last = make_calls()
    stick_row = stick_map.reshape(1, 128)
    land, full = big(
        occupations,
        block_place,
        block_atom,
        block_place.reshape(1, NBLK),
        block_atom.reshape(1, NBLK),
        stick_row,
        coupling,
        local_potential,
        wave_coef,
        tables["z_ahead"],
        tables["x_ahead"],
        tables["y_ahead"],
        projectors,
        tables["x_back"],
        tables["y_back"],
    )
    return last(stick_row, land, full, core_density, wave_coef, tables["z_back"])


def solution(mesh):
    tables = {name: jnp.asarray(value) for name, value in make_tables().items()}

    def run(*args):
        return local(tables, *args)

    return jax.shard_map(
        run,
        mesh=mesh,
        in_specs=(
            P(None, "band", None, "fft"),
            P("fft"),
            P("fft", None),
            P("fft", None),
            P("band"),
            P("fft"),
            P("fft"),
            P("fft", None, None),
            P(),
        ),
        out_specs=(P(None, "band", None, "fft"), P("fft", None), P("fft", None)),
        check_vma=False,
    )
```

```python
import math

import jax
import jax.numpy as jnp
import numpy as np
from jax import lax
from jax.experimental import pallas as pl
from jax.experimental.pallas import tpu as pltpu
from jax.sharding import PartitionSpec as P

N = 160
ZP = 3
N_FFT = 64
NBLK = 96
ATOM_DEV = 16
ATOMS = 1024
BANDS_AXIS = 4
SLICE = 152
SHIFT = 52
BOX = 104
HALF = 56
F32 = jnp.float32
BF16 = jnp.bfloat16

lda_factor = (3.0 / math.pi) ** (1.0 / 3.0)


def parts(table):
    high = table.astype(np.float32).astype(jnp.bfloat16)
    low = (table - high.astype(np.float64)).astype(np.float32).astype(jnp.bfloat16)
    return high, low


def real_form(cosine, sine):
    return np.block([[cosine, -sine], [sine, cosine]])


def z_tables():
    slot, place = np.meshgrid(np.arange(8), np.arange(N_FFT), indexing="ij")
    out = np.zeros((N_FFT, 8, 2, N))
    g = np.arange(N)
    for f in range(N_FFT):
        for s in range(ZP):
            z = s * N_FFT + f
            if z < N:
                phase = 2 * np.pi / N * ((z * g) % N)
                c, d = np.cos(phase) / math.sqrt(N), np.sin(phase) / math.sqrt(N)
                out[f, s, 0], out[f, s, 1] = c, -d
                out[f, 3 + s, 0], out[f, 3 + s, 1] = d, c
    forward = out.reshape(N_FFT * 8, 2 * N)
    return forward, forward.T


def x_tables():
    rows = np.array([4 * k + g for g in range(4) for k in range(40)])
    compact = np.array([2 * h + p for p in range(2) for h in range(HALF)])
    phase = 2 * np.pi / N * ((rows[:, None] * (compact[None, :] - SHIFT)) % N)
    keep = (compact < BOX)[None, :] / math.sqrt(N)
    ahead = real_form(np.cos(phase) * keep, np.sin(phase) * keep)
    phase = phase.T
    keep = keep.T
    back = real_form(np.cos(phase) * keep, -np.sin(phase) * keep)
    return ahead, back


PAIRS = tuple((j, g) for g in range(4) for j in (g, g + 1))


def y_tables():
    compact = np.arange(128)
    out = []
    for j, g in PAIRS:
        flat = 128 * j + np.arange(128)
        keep = ((flat // N == g)[None, :] & (compact < BOX)[:, None]) / math.sqrt(N)
        phase = 2 * np.pi / N * (((compact[:, None] - SHIFT) * (flat % N)[None, :]) % N)
        c, d = np.cos(phase) * keep, np.sin(phase) * keep
        out.append(np.block([[c, d], [-d, c]]))
    return np.stack(out)


def stack3(table, axis):
    high, low = parts(table)
    return np.concatenate([high, low, high], axis=axis)


def make_tables():
    z_ahead, z_back = z_tables()
    x_ahead, x_back = x_tables()
    y_ahead = y_tables()
    y_back = np.swapaxes(y_ahead, 1, 2)
    return dict(
        z_ahead=stack3(z_ahead, 1),
        z_back=stack3(z_back, 1),
        x_ahead=stack3(x_ahead, 1),
        x_back=stack3(x_back, 1),
        y_ahead=np.stack(parts(y_ahead), axis=1),
        y_back=np.stack(parts(y_back), axis=1),
    )


def split(value):
    high = value.astype(BF16)
    return high, (value - high.astype(F32)).astype(BF16)


def dot(left, right):
    return lax.dot_general(left, right, (((1,), (0,)), ((), ())), preferred_element_type=F32)


def dot_nt(left, right):
    return lax.dot_general(left, right, (((1,), (1,)), ((), ())), preferred_element_type=F32)


def lhs3(value):
    high, low = split(value)
    return jnp.concatenate([high, high, low], axis=1)


def rhs3(value):
    high, low = split(value)
    return jnp.concatenate([high, high, low], axis=0)


def grid_xy(stick_ref):
    column = stick_ref[...].astype(F32)
    x = jnp.floor((column + 0.5) * (1.0 / N))
    y = column - N * x
    return x, y


def block_row(place):
    slot = (place >= 200).astype(jnp.int32) + (place >= 400).astype(jnp.int32)
    inside = place - 200 * slot
    fifth = (inside * 6554) >> 15
    return slot * 200 + (inside - 5 * fifth) * 40 + fifth


ROWS = [(b, o, s) for b in range(2) for o in range(2) for s in range(ZP)]
CHUNK = 4
UNROLL_S = 4
UNROLL_G = 8
PART = 12 * HALF


def ahead_of(me, step):
    return lax.rem(me + step, N_FFT)


def behind(me, step):
    return lax.rem(me + N_FFT - step, N_FFT)


def fft_copy(source, target, send_sem, recv_sem, device):
    return pltpu.make_async_remote_copy(
        src_ref=source,
        dst_ref=target,
        send_sem=send_sem,
        recv_sem=recv_sem,
        device_id={"fft": device},
        device_id_type=pl.DeviceIdType.MESH,
    )


def band_copy(source, target, send_sem, recv_sem, device):
    return pltpu.make_async_remote_copy(
        src_ref=source,
        dst_ref=target,
        send_sem=send_sem,
        recv_sem=recv_sem,
        device_id={"band": device},
        device_id_type=pl.DeviceIdType.MESH,
    )


def put(send_ref, land_ref, send_sem, recv_sem, me, step):
    target = ahead_of(me, step)
    return fft_copy(send_ref.at[target], land_ref.at[me], send_sem, recv_sem, target)


def bytes_of(ref, count, sem):
    return pltpu.make_async_copy(ref.at[pl.ds(0, count)], ref.at[pl.ds(0, count)], sem)


def in_groups(body, count, group):
    for i in range(group):
        body(i)

    def one(at, carry):
        for i in range(group):
            body(at * group + i)
        return carry

    if count > group:
        lax.fori_loop(1, count // group, one, 0)


def whole(
    occ_ref,
    place_ref,
    atom_ref,
    place_row_ref,
    atom_row_ref,
    stick_ref,
    coupling_ref,
    potential_ref,
    wave_hbm,
    ztab_hbm,
    xtab_hbm,
    ytab_hbm,
    proj_hbm,
    xback_hbm,
    yback_hbm,
    land_ref,
    full_ref,
    wave_ref,
    ztab_ref,
    xtab_ref,
    ytab_ref,
    proj_ref,
    xback_ref,
    yback_ref,
    send_ref,
    first_ref,
    last_ref,
    grid_ref,
    mid_ref,
    psi_ref,
    power_ref,
    piece_ref,
    sums_ref,
    before_ref,
    after_ref,
    weight_ref,
    pot_ref,
    add_ref,
    h_ref,
    left_ref,
    part_ref,
    mine_ref,
    total_ref,
    sems,
    send_sems,
    recv_sems,
    halo_send_sems,
    halo_recv_sems,
    band_send_sems,
    band_recv_sems,
):
    me = lax.axis_index("fft")
    group = lax.axis_index("band")
    barrier = pltpu.get_barrier_semaphore()
    loads = [
        pltpu.make_async_copy(source, target, sems.at[i])
        for i, (source, target) in enumerate(
            [
                (wave_hbm, wave_ref),
                (ztab_hbm, ztab_ref),
                (xtab_hbm, xtab_ref),
                (ytab_hbm, ytab_ref),
                (proj_hbm, proj_ref),
                (xback_hbm, xback_ref),
                (yback_hbm, yback_ref),
            ]
        )
    ]
    for load in loads:
        load.start()

    def greet(step, carry):
        pl.semaphore_signal(
            barrier,
            inc=1,
            device_id={"fft": ahead_of(me, step)},
            device_id_type=pl.DeviceIdType.MESH,
        )
        return carry

    lax.fori_loop(1, N_FFT, greet, 0, unroll=3)
    for step in range(1, 4):
        pl.semaphore_signal(
            barrier,
            inc=1,
            device_id={"band": lax.rem(group + step, 4)},
            device_id_type=pl.DeviceIdType.MESH,
        )

    grid_ref[...] = jnp.zeros_like(grid_ref)
    x, y = grid_xy(stick_ref)
    half = N // 2
    xc = jnp.where(x < half, x, x - N) + SHIFT
    yc = jnp.where(y < half, y, y - N) + SHIFT
    loads[0].wait()
    loads[1].wait()
    both = [jnp.concatenate([wave_ref[0, b], wave_ref[1, b]], axis=0) for b in range(2)]
    result = dot(ztab_ref[...], rhs3(jnp.concatenate(both, axis=1)))
    for b in range(2):
        send_ref[:, 8 * b : 8 * b + 8, :] = result[:, 128 * b : 128 * b + 128].reshape(
            N_FFT, 8, 128
        )
    send_ref[:, 6:7, :] = jnp.broadcast_to(xc[None], (N_FFT, 1, 128))
    send_ref[:, 7:8, :] = jnp.broadcast_to(yc[None], (N_FFT, 1, 128))

    pl.semaphore_wait(barrier, N_FFT - 1 + 3)

    def send(step, carry):
        chunk = lax.div(step, CHUNK)
        put(send_ref, first_ref, send_sems.at[0], recv_sems.at[chunk], me, step).start()
        return carry

    lax.fori_loop(1, N_FFT, send, 0, unroll=3)
    first_ref[me] = send_ref[me]

    row_id = lax.broadcasted_iota(jnp.int32, (HALF, 128), 0).astype(F32)
    lane_id = lax.broadcasted_iota(jnp.int32, (256, 128), 0).astype(F32)

    def scatter(chunk):
        own = 1 if isinstance(chunk, int) and chunk == 0 else 0
        bytes_of(first_ref, CHUNK - own, recv_sems.at[chunk]).wait()
        lefts, rights = [], []
        for i in range(CHUNK):
            step = chunk * CHUNK + i
            tile = first_ref[behind(me, step)]
            x, y = tile[6:7], tile[7:8]
            x2 = jnp.floor(x * 0.5)
            here = row_id == x2
            rights.append((lane_id == (x - 2.0 * x2) * 128.0 + y).astype(F32).astype(BF16))
            high = tile.astype(BF16).astype(F32)
            picked = [
                jnp.where(here, piece[8 * b + 3 * o + s : 8 * b + 3 * o + s + 1], 0.0)
                for piece in (high, tile - high)
                for b, o, s in ROWS
            ]
            lefts.append(jnp.concatenate(picked, axis=0).astype(BF16))
        grid_ref[...] += dot_nt(jnp.concatenate(lefts, axis=1), jnp.concatenate(rights, axis=1))

    in_groups(scatter, N_FFT // CHUNK, UNROLL_S)

    columns = []
    for b in range(2):
        for s in range(ZP):
            rows = []
            for o in range(2):
                first = (b * 6 + o * 3 + s) * HALF
                for parity in range(2):
                    lanes = slice(128 * parity, 128 * parity + 128)
                    rows.append(
                        grid_ref[first : first + HALF, lanes]
                        + grid_ref[PART + first : PART + first + HALF, lanes]
                    )
            columns.append(jnp.concatenate(rows, axis=0))
    loads[2].wait()
    mixed = dot(xtab_ref[...], rhs3(jnp.concatenate(columns, axis=1)))
    for g in range(4):
        for o in range(2):
            first = (o * 4 + g) * 40
            for bs in range(6):
                mid_ref[g, 40 * bs : 40 * bs + 40, 128 * o : 128 * o + 128] = mixed[
                    first : first + 40, 128 * bs : 128 * bs + 128
                ]
    lefts = [lhs3(mid_ref[g]) for g in range(4)]
    loads[3].wait()
    for j in range(5):
        total = None
        for at, (tile, g) in enumerate(PAIRS):
            if tile == j:
                high, low = ytab_ref[at, 0], ytab_ref[at, 1]
                term = dot(lefts[g], jnp.concatenate([high, low, high], axis=0))
                total = term if total is None else total + term
        for b in range(2):
            for s in range(ZP):
                bs = b * ZP + s
                for o in range(2):
                    first = s * 200 + j * 40
                    psi_ref[b * 2 + o, first : first + 40, :] = total[
                        40 * bs : 40 * bs + 40, 128 * o : 128 * o + 128
                    ]

    def power(b):
        re, im = psi_ref[2 * b], psi_ref[2 * b + 1]
        return re * re + im * im

    power_ref[:600] = occ_ref[0] * power(0) + occ_ref[1] * power(1)
    power_ref[600:] = jnp.zeros((4 * SLICE - 600, 128), F32)

    def rows_of(index):
        return pl.ds(pl.multiple_of(index * SLICE, 8), SLICE)

    def quarter(step):
        target = lax.rem(group + step, 4)
        return band_copy(
            power_ref.at[rows_of(target)],
            part_ref.at[step - 1],
            band_send_sems.at[step - 1],
            band_recv_sems.at[step - 1],
            target,
        )

    for step in range(1, 4):
        quarter(step).start()

    def fetch(k, carry):
        row = block_row(place_ref[k])
        for c in range(4):
            piece_ref[pl.ds(4 * k + c, 1), :] = psi_ref[c, pl.ds(row, 1), :]
        return carry

    lax.fori_loop(0, NBLK, fetch, 0, unroll=4)
    loads[4].wait()
    lane = lax.broadcasted_iota(jnp.int32, (64, 128), 1)
    picks = []
    for part in range(3):
        piece_high, piece_low = split(piece_ref[128 * part : 128 * part + 128])
        piece_both = jnp.concatenate([piece_high, piece_high], axis=1)
        found = jnp.zeros((64, 128), F32)
        for chunk in range(2):
            first = part * 32 + chunk * 16
            high, low = split(proj_ref[first : first + 16].reshape(1024, 128))
            values = dot_nt(jnp.concatenate([high, low], axis=1), piece_both)
            values = values + dot_nt(high, piece_low)
            for m in range(16):
                own = lax.div(lane, 4) == chunk * 16 + m
                found = jnp.where(own, values[64 * m : 64 * m + 64], found)
        picks.append(found)
    found = jnp.concatenate(picks, axis=1)
    base = me * ATOM_DEV - ATOM_DEV // 2
    near = lax.rem(atom_row_ref[...] - base + 2 * ATOMS, ATOMS).astype(F32)
    spread = lax.div(lax.broadcasted_iota(jnp.int32, (NBLK, 4 * NBLK), 1), 4)
    spread = spread == lax.broadcasted_iota(jnp.int32, (NBLK, 4 * NBLK), 0)
    near = dot(
        jnp.broadcast_to(near, (16, NBLK)).astype(BF16), spread.astype(F32).astype(BF16)
    )[0:1]
    column = lax.broadcasted_iota(jnp.int32, (128, 4 * NBLK), 0)
    owner = lax.rem(lax.broadcasted_iota(jnp.int32, (128, 4 * NBLK), 1), 4).astype(F32) + 4.0 * near
    member = (owner == column.astype(F32)).astype(F32).astype(BF16)
    high, low = split(found)
    sums_ref[...] = dot_nt(
        jnp.concatenate([high, low], axis=1), jnp.concatenate([member, member], axis=1)
    )
    after_me, before_me = ahead_of(me, 1), behind(me, 1)
    to_after = fft_copy(
        sums_ref, before_ref, halo_send_sems.at[0], halo_recv_sems.at[0], after_me
    )
    to_before = fft_copy(
        sums_ref, after_ref, halo_send_sems.at[1], halo_recv_sems.at[1], before_me
    )
    to_after.start()
    to_before.start()

    for q in range(200):
        row = (q % 5) * 40 + q // 5
        pot_ref[:, row, :] = potential_ref[:, 128 * q : 128 * q + 128]

    for step in range(1, 4):
        quarter(step).wait()
    mine_ref[...] = power_ref[rows_of(group)] + part_ref[0] + part_ref[1] + part_ref[2]
    total_ref[rows_of(group)] = mine_ref[...]

    def share(step):
        return band_copy(
            mine_ref,
            total_ref.at[rows_of(group)],
            band_send_sems.at[2 + step],
            band_recv_sems.at[2 + step],
            lax.rem(group + step, 4),
        )

    for step in range(1, 4):
        share(step).start()

    to_after.wait()
    to_before.wait()
    beside = jnp.where(
        lane < 64, pltpu.roll(before_ref[...], 64, 1), pltpu.roll(after_ref[...], 64, 1)
    )
    weight = lax.dot_general(
        coupling_ref[...],
        sums_ref[...] + beside,
        (((1,), (0,)), ((), ())),
        precision=lax.Precision.HIGHEST,
        preferred_element_type=F32,
    )
    for n in range(128):
        weight_ref[n] = jnp.broadcast_to(weight[:, n : n + 1], (64, 128))

    def added(k, carry):
        first = ((atom_ref[k] - base) & (2 * ATOM_DEV - 1)) * 4
        values = proj_ref[k]
        for c in range(4):
            add_ref[c, pl.ds(k, 1), :] = jnp.sum(
                values * weight_ref[first + c], axis=0, keepdims=True
            )
        return carry

    lax.fori_loop(0, NBLK, added, 0, unroll=2)
    place = place_row_ref[...]
    slot = (place >= 200).astype(jnp.int32) + (place >= 400).astype(jnp.int32)
    inside = place - 200 * slot
    fifth = (inside * 6554) >> 15
    place = slot * 200 + (inside - 5 * fifth) * 40 + fifth
    block_id = lax.broadcasted_iota(jnp.int32, (600, NBLK), 0)
    spot = (block_id == place).astype(F32).astype(BF16)
    potential = pot_ref[...].reshape(600, 128)
    for c in range(4):
        high, low = split(add_ref[c])
        h_ref[c] = potential * psi_ref[c] + (dot(spot, high) + dot(spot, low))

    lefts = []
    for j in range(5):
        rows = []
        for b in range(2):
            for s in range(ZP):
                first = s * 200 + j * 40
                rows.append(
                    jnp.concatenate(
                        [h_ref[b * 2 + o, first : first + 40, :] for o in range(2)], axis=1
                    )
                )
        lefts.append(lhs3(jnp.concatenate(rows, axis=0)))
    loads[6].wait()
    turned = []
    for g in range(4):
        total = None
        for at, (j, owner) in enumerate(PAIRS):
            if owner == g:
                high, low = yback_ref[at, 0], yback_ref[at, 1]
                term = dot(lefts[j], jnp.concatenate([high, low, high], axis=0))
                total = term if total is None else total + term
        turned.append(total)
    columns = []
    for bs in range(6):
        rows = []
        for o in range(2):
            for g in range(4):
                rows.append(turned[g][40 * bs : 40 * bs + 40, 128 * o : 128 * o + 128])
        columns.append(jnp.concatenate(rows, axis=0))
    loads[5].wait()
    spectrum = dot(xback_ref[...], rhs3(jnp.concatenate(columns, axis=1)))
    for at, (b, o, s) in enumerate(ROWS):
        bs = b * ZP + s
        for parity in range(2):
            first = (o * 2 + parity) * HALF
            grid_ref[at * HALF : at * HALF + HALF, 128 * parity : 128 * parity + 128] = spectrum[
                first : first + HALF, 128 * bs : 128 * bs + 128
            ]
    high, low = split(grid_ref[:PART])
    left_ref[:PART] = high
    left_ref[PART:] = low

    id256 = lax.broadcasted_iota(jnp.int32, (256, 256), 0).astype(F32)
    zeros = jnp.zeros((2, 256), F32)

    def gather(pair):
        steps = (2 * pair, 2 * pair + 1)
        targets = [ahead_of(me, step) for step in steps]
        tiles = [first_ref[target, 0:8, :] for target in targets]
        x = jnp.concatenate([tile[6:7] for tile in tiles], axis=1)
        y = jnp.concatenate([tile[7:8] for tile in tiles], axis=1)
        x2 = jnp.floor(x * 0.5)
        here = id256[:HALF] == x2
        spot = (id256 == (x - 2.0 * x2) * 128.0 + y).astype(F32).astype(BF16)
        values = dot(left_ref[...], spot)
        rows = []
        for at in range(12):
            first = at * HALF
            one = values[first : first + HALF] + values[PART + first : PART + first + HALF]
            rows.append(jnp.sum(jnp.where(here, one, 0.0), axis=0, keepdims=True))
            if at % 6 == 5:
                rows.append(zeros)
        result = jnp.concatenate(rows, axis=0)
        for i in range(2):
            send2_ref[targets[i]] = result[:, 128 * i : 128 * i + 128]

        for step in steps:
            if not isinstance(step, int) or step > 0:
                put(send2_ref, last_ref, send_sems.at[1], send_sems.at[2], me, step).start()

    bytes_of(send_ref, N_FFT - 1, send_sems.at[0]).wait()
    send2_ref = send_ref
    in_groups(gather, N_FFT // 2, UNROLL_G)
    last_ref[me] = send2_ref[me]

    for step in range(1, 4):
        source = lax.rem(group + 4 - step, 4)
        band_copy(
            mine_ref,
            total_ref.at[rows_of(source)],
            band_send_sems.at[2 + step],
            band_recv_sems.at[2 + step],
            source,
        ).wait_recv()
    for step in range(1, 4):
        share(step).wait_send()
    full_ref[...] = total_ref[...]

    bytes_of(last_ref, N_FFT - 1, send_sems.at[2]).wait()
    land_ref[...] = last_ref[...]
    bytes_of(send2_ref, N_FFT - 1, send_sems.at[1]).wait()


def finish(
    stick_ref,
    land_ref,
    full_ref,
    core_ref,
    wave_ref,
    ztab_ref,
    out_ref,
    dens_ref,
    field_ref,
    box_ref,
    core3_ref,
):
    me = lax.axis_index("fft")
    for q in range(200):
        row = (q % 5) * 40 + q // 5
        core3_ref[:, row, :] = core_ref[:, 128 * q : 128 * q + 128]
    density = full_ref[:600].reshape(ZP, 200, 128)
    box_ref[...] = density
    for q in range(200):
        row = (q % 5) * 40 + q // 5
        dens_ref[:, 128 * q : 128 * q + 128] = box_ref[:, row, :]
    slot = lax.broadcasted_iota(jnp.int32, (ZP, 200, 128), 0)
    field = -lda_factor * jnp.exp(jnp.log(density + core3_ref[...]) * (1.0 / 3.0))
    core3_ref[...] = jnp.where(slot * N_FFT + me < N, field, 0.0)
    for q in range(200):
        row = (q % 5) * 40 + q // 5
        field_ref[:, 128 * q : 128 * q + 128] = core3_ref[:, row, :]
    x, y = grid_xy(stick_ref)
    half = N // 2
    x = jnp.where(x < half, x, x - N) / N
    y = jnp.where(y < half, y, y - N) / N
    g = lax.broadcasted_iota(jnp.int32, (N, 128), 0)
    z = jnp.where(g < half, g, g - N).astype(F32) / N
    kinetic = 2.0 * (x * x + y * y) + 2.0 * (z * z)
    both = [land_ref[:, 8 * b : 8 * b + 8, :].reshape(N_FFT * 8, 128) for b in range(2)]
    result = dot(ztab_ref[...], rhs3(jnp.concatenate(both, axis=1)))
    for o in range(2):
        for b in range(2):
            spectrum = result[N * o : N * o + N, 128 * b : 128 * b + 128]
            out_ref[o, b] = spectrum + kinetic * wave_ref[o, b]


VMEM = pltpu.VMEM
DMA = pltpu.SemaphoreType.DMA
SMEM_SPEC = pl.BlockSpec(memory_space=pltpu.SMEM)
VMEM_SPEC = pl.BlockSpec(memory_space=pltpu.VMEM)
ANY_SPEC = pl.BlockSpec(memory_space=pl.ANY)
LIMIT = 56 * 1024 * 1024


def call(body, in_specs, outs, scratch=(), flops=0, size=0, remote=None):
    options = {} if remote is None else dict(collective_id=remote, has_side_effects=True)
    return pl.pallas_call(
        body,
        out_shape=outs,
        in_specs=in_specs,
        out_specs=jax.tree.map(lambda _: VMEM_SPEC, outs),
        scratch_shapes=list(scratch),
        compiler_params=pltpu.CompilerParams(vmem_limit_bytes=LIMIT, **options),
        cost_estimate=pl.CostEstimate(flops=flops, bytes_accessed=size, transcendentals=0),
    )


def shape(*dims):
    return jax.ShapeDtypeStruct(dims, F32)


def make_calls():
    ytab = VMEM((8, 2, 256, 256), BF16)
    tiles = VMEM((N_FFT, 16, 128), F32)
    block = VMEM((64, 128), F32)
    big = call(
        whole,
        [SMEM_SPEC] * 3 + [VMEM_SPEC] * 5 + [ANY_SPEC] * 7,
        (shape(N_FFT, 16, 128), shape(4 * SLICE, 128)),
        (
            VMEM((2, 2, N, 128), F32),
            VMEM((8 * N_FFT, 6 * N), BF16),
            VMEM((2 * N, 12 * HALF), BF16),
            ytab,
            VMEM((NBLK, 64, 128), F32),
            VMEM((4 * HALF, 6 * N), BF16),
            ytab,
            tiles,
            tiles,
            tiles,
            VMEM((2 * PART, 256), F32),
            VMEM((4, 240, 256), F32),
            VMEM((4, 600, 128), F32),
            VMEM((4 * SLICE, 128), F32),
            VMEM((4 * NBLK, 128), F32),
            block,
            block,
            block,
            VMEM((128, 64, 128), F32),
            VMEM((ZP, 200, 128), F32),
            VMEM((4, NBLK, 128), F32),
            VMEM((4, 600, 128), F32),
            VMEM((2 * PART, 256), BF16),
            VMEM((3, SLICE, 128), F32),
            VMEM((SLICE, 128), F32),
            VMEM((4 * SLICE, 128), F32),
            DMA((7,)),
            DMA((3,)),
            DMA((N_FFT // CHUNK,)),
            DMA((2,)),
            DMA((2,)),
            DMA((6,)),
            DMA((6,)),
        ),
        20_000_000_000,
        16_000_000,
        0,
    )
    last = call(
        finish,
        [VMEM_SPEC] * 6,
        (shape(2, 2, N, 128), shape(ZP, N * N), shape(ZP, N * N)),
        (VMEM((ZP, 200, 128), F32), VMEM((ZP, 200, 128), F32)),
        500_000_000,
        4_000_000,
    )
    return big, last


def local(
    tables,
    wave_coef,
    stick_map,
    local_potential,
    core_density,
    occupations,
    block_place,
    block_atom,
    projectors,
    coupling,
):
    big, last = make_calls()
    stick_row = stick_map.reshape(1, 128)
    land, full = big(
        occupations,
        block_place,
        block_atom,
        block_place.reshape(1, NBLK),
        block_atom.reshape(1, NBLK),
        stick_row,
        coupling,
        local_potential,
        wave_coef,
        tables["z_ahead"],
        tables["x_ahead"],
        tables["y_ahead"],
        projectors,
        tables["x_back"],
        tables["y_back"],
    )
    return last(stick_row, land, full, core_density, wave_coef, tables["z_back"])


def solution(mesh):
    tables = {name: jnp.asarray(value) for name, value in make_tables().items()}

    def run(*args):
        return local(tables, *args)

    return jax.shard_map(
        run,
        mesh=mesh,
        in_specs=(
            P(None, "band", None, "fft"),
            P("fft"),
            P("fft", None),
            P("fft", None),
            P("band"),
            P("fft"),
            P("fft"),
            P("fft", None, None),
            P(),
        ),
        out_specs=(P(None, "band", None, "fft"), P("fft", None), P("fft", None)),
        check_vma=False,
    )
```

```python
import math

import jax
import jax.numpy as jnp
import numpy as np
from jax import lax
from jax.experimental import pallas as pl
from jax.experimental.pallas import tpu as pltpu
from jax.sharding import PartitionSpec as P

N = 160
ZP = 3
N_FFT = 64
NBLK = 96
ATOM_DEV = 16
ATOMS = 1024
BANDS_AXIS = 4
SLICE = 152
SHIFT = 52
BOX = 104
HALF = 56
F32 = jnp.float32
BF16 = jnp.bfloat16

lda_factor = (3.0 / math.pi) ** (1.0 / 3.0)


def parts(table):
    high = table.astype(np.float32).astype(jnp.bfloat16)
    low = (table - high.astype(np.float64)).astype(np.float32).astype(jnp.bfloat16)
    return high, low


def real_form(cosine, sine):
    return np.block([[cosine, -sine], [sine, cosine]])


def z_tables():
    slot, place = np.meshgrid(np.arange(8), np.arange(N_FFT), indexing="ij")
    out = np.zeros((N_FFT, 8, 2, N))
    g = np.arange(N)
    for f in range(N_FFT):
        for s in range(ZP):
            z = s * N_FFT + f
            if z < N:
                phase = 2 * np.pi / N * ((z * g) % N)
                c, d = np.cos(phase) / math.sqrt(N), np.sin(phase) / math.sqrt(N)
                out[f, s, 0], out[f, s, 1] = c, -d
                out[f, 3 + s, 0], out[f, 3 + s, 1] = d, c
    forward = out.reshape(N_FFT * 8, 2 * N)
    return forward, forward.T


def x_tables():
    rows = np.array([4 * k + g for g in range(4) for k in range(40)])
    compact = np.array([2 * h + p for p in range(2) for h in range(HALF)])
    phase = 2 * np.pi / N * ((rows[:, None] * (compact[None, :] - SHIFT)) % N)
    keep = (compact < BOX)[None, :] / math.sqrt(N)
    ahead = real_form(np.cos(phase) * keep, np.sin(phase) * keep)
    phase = phase.T
    keep = keep.T
    back = real_form(np.cos(phase) * keep, -np.sin(phase) * keep)
    return ahead, back


PAIRS = tuple((j, g) for g in range(4) for j in (g, g + 1))


def y_tables():
    compact = np.arange(128)
    out = []
    for j, g in PAIRS:
        flat = 128 * j + np.arange(128)
        keep = ((flat // N == g)[None, :] & (compact < BOX)[:, None]) / math.sqrt(N)
        phase = 2 * np.pi / N * (((compact[:, None] - SHIFT) * (flat % N)[None, :]) % N)
        c, d = np.cos(phase) * keep, np.sin(phase) * keep
        out.append(np.block([[c, d], [-d, c]]))
    return np.stack(out)


def stack3(table, axis):
    high, low = parts(table)
    return np.concatenate([high, low, high], axis=axis)


def make_tables():
    z_ahead, z_back = z_tables()
    x_ahead, x_back = x_tables()
    y_ahead = y_tables()
    y_back = np.swapaxes(y_ahead, 1, 2)
    return dict(
        z_ahead=stack3(z_ahead, 1),
        z_back=stack3(z_back, 1),
        x_ahead=stack3(x_ahead, 1),
        x_back=stack3(x_back, 1),
        y_ahead=np.stack(parts(y_ahead), axis=1),
        y_back=np.stack(parts(y_back), axis=1),
    )


def split(value):
    high = value.astype(BF16)
    return high, (value - high.astype(F32)).astype(BF16)


def dot(left, right):
    return lax.dot_general(left, right, (((1,), (0,)), ((), ())), preferred_element_type=F32)


def dot_nt(left, right):
    return lax.dot_general(left, right, (((1,), (1,)), ((), ())), preferred_element_type=F32)


def lhs3(value):
    high, low = split(value)
    return jnp.concatenate([high, high, low], axis=1)


def rhs3(value):
    high, low = split(value)
    return jnp.concatenate([high, high, low], axis=0)


def grid_xy(stick_ref):
    column = stick_ref[...].astype(F32)
    x = jnp.floor((column + 0.5) * (1.0 / N))
    y = column - N * x
    return x, y


def block_row(place):
    slot = (place >= 200).astype(jnp.int32) + (place >= 400).astype(jnp.int32)
    inside = place - 200 * slot
    fifth = (inside * 6554) >> 15
    return slot * 200 + (inside - 5 * fifth) * 40 + fifth


ROWS = [(b, o, s) for b in range(2) for o in range(2) for s in range(ZP)]
CHUNK = 4
UNROLL_S = 2
UNROLL_G = 4
PART = 12 * HALF


def ahead_of(me, step):
    return lax.rem(me + step, N_FFT)


def behind(me, step):
    return lax.rem(me + N_FFT - step, N_FFT)


def fft_copy(source, target, send_sem, recv_sem, device):
    return pltpu.make_async_remote_copy(
        src_ref=source,
        dst_ref=target,
        send_sem=send_sem,
        recv_sem=recv_sem,
        device_id={"fft": device},
        device_id_type=pl.DeviceIdType.MESH,
    )


def band_copy(source, target, send_sem, recv_sem, device):
    return pltpu.make_async_remote_copy(
        src_ref=source,
        dst_ref=target,
        send_sem=send_sem,
        recv_sem=recv_sem,
        device_id={"band": device},
        device_id_type=pl.DeviceIdType.MESH,
    )


def put(send_ref, land_ref, send_sem, recv_sem, me, step):
    target = ahead_of(me, step)
    return fft_copy(send_ref.at[target], land_ref.at[me], send_sem, recv_sem, target)


def bytes_of(ref, count, sem):
    return pltpu.make_async_copy(ref.at[pl.ds(0, count)], ref.at[pl.ds(0, count)], sem)


def whole(
    occ_ref,
    place_ref,
    atom_ref,
    place_row_ref,
    atom_row_ref,
    stick_ref,
    coupling_ref,
    potential_ref,
    wave_hbm,
    ztab_hbm,
    xtab_hbm,
    ytab_hbm,
    proj_hbm,
    xback_hbm,
    yback_hbm,
    land_ref,
    full_ref,
    wave_ref,
    ztab_ref,
    xtab_ref,
    ytab_ref,
    proj_ref,
    xback_ref,
    yback_ref,
    send_ref,
    first_ref,
    last_ref,
    grid_ref,
    mid_ref,
    psi_ref,
    power_ref,
    piece_ref,
    sums_ref,
    before_ref,
    after_ref,
    weight_ref,
    pot_ref,
    add_ref,
    h_ref,
    left_ref,
    part_ref,
    mine_ref,
    total_ref,
    sems,
    send_sems,
    recv_sems,
    halo_send_sems,
    halo_recv_sems,
    band_send_sems,
    band_recv_sems,
):
    me = lax.axis_index("fft")
    group = lax.axis_index("band")
    barrier = pltpu.get_barrier_semaphore()
    loads = [
        pltpu.make_async_copy(source, target, sems.at[i])
        for i, (source, target) in enumerate(
            [
                (wave_hbm, wave_ref),
                (ztab_hbm, ztab_ref),
                (xtab_hbm, xtab_ref),
                (ytab_hbm, ytab_ref),
                (proj_hbm, proj_ref),
                (xback_hbm, xback_ref),
                (yback_hbm, yback_ref),
            ]
        )
    ]
    for load in loads:
        load.start()

    def greet(step, carry):
        pl.semaphore_signal(
            barrier,
            inc=1,
            device_id={"fft": ahead_of(me, step)},
            device_id_type=pl.DeviceIdType.MESH,
        )
        return carry

    lax.fori_loop(1, N_FFT, greet, 0, unroll=3)
    for step in range(1, 4):
        pl.semaphore_signal(
            barrier,
            inc=1,
            device_id={"band": lax.rem(group + step, 4)},
            device_id_type=pl.DeviceIdType.MESH,
        )

    grid_ref[...] = jnp.zeros_like(grid_ref)
    x, y = grid_xy(stick_ref)
    half = N // 2
    xc = jnp.where(x < half, x, x - N) + SHIFT
    yc = jnp.where(y < half, y, y - N) + SHIFT
    loads[0].wait()
    loads[1].wait()
    both = [jnp.concatenate([wave_ref[0, b], wave_ref[1, b]], axis=0) for b in range(2)]
    result = dot(ztab_ref[...], rhs3(jnp.concatenate(both, axis=1)))
    for b in range(2):
        send_ref[:, 8 * b : 8 * b + 8, :] = result[:, 128 * b : 128 * b + 128].reshape(
            N_FFT, 8, 128
        )
    send_ref[:, 6:7, :] = jnp.broadcast_to(xc[None], (N_FFT, 1, 128))
    send_ref[:, 7:8, :] = jnp.broadcast_to(yc[None], (N_FFT, 1, 128))

    pl.semaphore_wait(barrier, N_FFT - 1 + 3)

    def send(step, carry):
        chunk = lax.div(step, CHUNK)
        put(send_ref, first_ref, send_sems.at[0], recv_sems.at[chunk], me, step).start()
        return carry

    lax.fori_loop(1, N_FFT, send, 0, unroll=3)
    pltpu.make_async_copy(send_ref.at[me], first_ref.at[me], recv_sems.at[0]).start()

    row_id = lax.broadcasted_iota(jnp.int32, (HALF, 128), 0).astype(F32)
    lane_id = lax.broadcasted_iota(jnp.int32, (256, 128), 0).astype(F32)

    def scatter(chunk):
        lefts, rights = [], []
        for i in range(CHUNK):
            step = chunk * CHUNK + i
            tile = first_ref[behind(me, step)]
            x, y = tile[6:7], tile[7:8]
            x2 = jnp.floor(x * 0.5)
            here = row_id == x2
            rights.append((lane_id == (x - 2.0 * x2) * 128.0 + y).astype(F32).astype(BF16))
            high = tile.astype(BF16).astype(F32)
            picked = [
                jnp.where(here, piece[8 * b + 3 * o + s : 8 * b + 3 * o + s + 1], 0.0)
                for piece in (high, tile - high)
                for b, o, s in ROWS
            ]
            lefts.append(jnp.concatenate(picked, axis=0).astype(BF16))
        grid_ref[...] += dot_nt(jnp.concatenate(lefts, axis=1), jnp.concatenate(rights, axis=1))

    def scatter_group(at, carry):
        for i in range(UNROLL_S):
            bytes_of(first_ref, CHUNK, recv_sems.at[at * UNROLL_S + i]).wait()
        for i in range(UNROLL_S):
            scatter(at * UNROLL_S + i)
        return carry

    lax.fori_loop(0, N_FFT // CHUNK // UNROLL_S, scatter_group, 0)

    columns = []
    for b in range(2):
        for s in range(ZP):
            rows = []
            for o in range(2):
                first = (b * 6 + o * 3 + s) * HALF
                for parity in range(2):
                    lanes = slice(128 * parity, 128 * parity + 128)
                    rows.append(
                        grid_ref[first : first + HALF, lanes]
                        + grid_ref[PART + first : PART + first + HALF, lanes]
                    )
            columns.append(jnp.concatenate(rows, axis=0))
    loads[2].wait()
    mixed = dot(xtab_ref[...], rhs3(jnp.concatenate(columns, axis=1)))
    for g in range(4):
        for o in range(2):
            first = (o * 4 + g) * 40
            for bs in range(6):
                mid_ref[g, 40 * bs : 40 * bs + 40, 128 * o : 128 * o + 128] = mixed[
                    first : first + 40, 128 * bs : 128 * bs + 128
                ]
    lefts = [lhs3(mid_ref[g]) for g in range(4)]
    loads[3].wait()
    for j in range(5):
        total = None
        for at, (tile, g) in enumerate(PAIRS):
            if tile == j:
                high, low = ytab_ref[at, 0], ytab_ref[at, 1]
                term = dot(lefts[g], jnp.concatenate([high, low, high], axis=0))
                total = term if total is None else total + term
        for b in range(2):
            for s in range(ZP):
                bs = b * ZP + s
                for o in range(2):
                    first = s * 200 + j * 40
                    psi_ref[b * 2 + o, first : first + 40, :] = total[
                        40 * bs : 40 * bs + 40, 128 * o : 128 * o + 128
                    ]

    def power(b):
        re, im = psi_ref[2 * b], psi_ref[2 * b + 1]
        return re * re + im * im

    power_ref[:600] = occ_ref[0] * power(0) + occ_ref[1] * power(1)
    power_ref[600:] = jnp.zeros((4 * SLICE - 600, 128), F32)

    def rows_of(index):
        return pl.ds(pl.multiple_of(index * SLICE, 8), SLICE)

    def quarter(step):
        target = lax.rem(group + step, 4)
        return band_copy(
            power_ref.at[rows_of(target)],
            part_ref.at[step - 1],
            band_send_sems.at[step - 1],
            band_recv_sems.at[step - 1],
            target,
        )

    for step in range(1, 4):
        quarter(step).start()

    def fetch(k, carry):
        row = block_row(place_ref[k])
        for c in range(4):
            piece_ref[pl.ds(4 * k + c, 1), :] = psi_ref[c, pl.ds(row, 1), :]
        return carry

    lax.fori_loop(0, NBLK, fetch, 0, unroll=4)
    loads[4].wait()
    lane = lax.broadcasted_iota(jnp.int32, (64, 128), 1)
    picks = []
    for part in range(3):
        piece_high, piece_low = split(piece_ref[128 * part : 128 * part + 128])
        piece_both = jnp.concatenate([piece_high, piece_high], axis=1)
        found = jnp.zeros((64, 128), F32)
        for chunk in range(2):
            first = part * 32 + chunk * 16
            high, low = split(proj_ref[first : first + 16].reshape(1024, 128))
            values = dot_nt(jnp.concatenate([high, low], axis=1), piece_both)
            values = values + dot_nt(high, piece_low)
            for m in range(16):
                own = lax.div(lane, 4) == chunk * 16 + m
                found = jnp.where(own, values[64 * m : 64 * m + 64], found)
        picks.append(found)
    found = jnp.concatenate(picks, axis=1)
    base = me * ATOM_DEV - ATOM_DEV // 2
    near = lax.rem(atom_row_ref[...] - base + 2 * ATOMS, ATOMS).astype(F32)
    spread = lax.div(lax.broadcasted_iota(jnp.int32, (NBLK, 4 * NBLK), 1), 4)
    spread = spread == lax.broadcasted_iota(jnp.int32, (NBLK, 4 * NBLK), 0)
    near = dot(
        jnp.broadcast_to(near, (16, NBLK)).astype(BF16), spread.astype(F32).astype(BF16)
    )[0:1]
    column = lax.broadcasted_iota(jnp.int32, (128, 4 * NBLK), 0)
    owner = lax.rem(lax.broadcasted_iota(jnp.int32, (128, 4 * NBLK), 1), 4).astype(F32) + 4.0 * near
    member = (owner == column.astype(F32)).astype(F32).astype(BF16)
    high, low = split(found)
    sums_ref[...] = dot_nt(
        jnp.concatenate([high, low], axis=1), jnp.concatenate([member, member], axis=1)
    )
    after_me, before_me = ahead_of(me, 1), behind(me, 1)
    to_after = fft_copy(
        sums_ref, before_ref, halo_send_sems.at[0], halo_recv_sems.at[0], after_me
    )
    to_before = fft_copy(
        sums_ref, after_ref, halo_send_sems.at[1], halo_recv_sems.at[1], before_me
    )
    to_after.start()
    to_before.start()

    for q in range(200):
        row = (q % 5) * 40 + q // 5
        pot_ref[:, row, :] = potential_ref[:, 128 * q : 128 * q + 128]

    for step in range(1, 4):
        quarter(step).wait()
    mine_ref[...] = power_ref[rows_of(group)] + part_ref[0] + part_ref[1] + part_ref[2]
    total_ref[rows_of(group)] = mine_ref[...]

    def share(step):
        return band_copy(
            mine_ref,
            total_ref.at[rows_of(group)],
            band_send_sems.at[2 + step],
            band_recv_sems.at[2 + step],
            lax.rem(group + step, 4),
        )

    for step in range(1, 4):
        share(step).start()

    to_after.wait()
    to_before.wait()
    beside = jnp.where(
        lane < 64, pltpu.roll(before_ref[...], 64, 1), pltpu.roll(after_ref[...], 64, 1)
    )
    weight = lax.dot_general(
        coupling_ref[...],
        sums_ref[...] + beside,
        (((1,), (0,)), ((), ())),
        precision=lax.Precision.HIGHEST,
        preferred_element_type=F32,
    )
    for n in range(128):
        weight_ref[n] = jnp.broadcast_to(weight[:, n : n + 1], (64, 128))

    def added(k, carry):
        first = ((atom_ref[k] - base) & (2 * ATOM_DEV - 1)) * 4
        values = proj_ref[k]
        for c in range(4):
            add_ref[c, pl.ds(k, 1), :] = jnp.sum(
                values * weight_ref[first + c], axis=0, keepdims=True
            )
        return carry

    lax.fori_loop(0, NBLK, added, 0, unroll=2)
    place = place_row_ref[...]
    slot = (place >= 200).astype(jnp.int32) + (place >= 400).astype(jnp.int32)
    inside = place - 200 * slot
    fifth = (inside * 6554) >> 15
    place = slot * 200 + (inside - 5 * fifth) * 40 + fifth
    block_id = lax.broadcasted_iota(jnp.int32, (600, NBLK), 0)
    spot = (block_id == place).astype(F32).astype(BF16)
    potential = pot_ref[...].reshape(600, 128)
    for c in range(4):
        high, low = split(add_ref[c])
        h_ref[c] = potential * psi_ref[c] + (dot(spot, high) + dot(spot, low))

    lefts = []
    for j in range(5):
        rows = []
        for b in range(2):
            for s in range(ZP):
                first = s * 200 + j * 40
                rows.append(
                    jnp.concatenate(
                        [h_ref[b * 2 + o, first : first + 40, :] for o in range(2)], axis=1
                    )
                )
        lefts.append(lhs3(jnp.concatenate(rows, axis=0)))
    loads[6].wait()
    turned = []
    for g in range(4):
        total = None
        for at, (j, owner) in enumerate(PAIRS):
            if owner == g:
                high, low = yback_ref[at, 0], yback_ref[at, 1]
                term = dot(lefts[j], jnp.concatenate([high, low, high], axis=0))
                total = term if total is None else total + term
        turned.append(total)
    columns = []
    for bs in range(6):
        rows = []
        for o in range(2):
            for g in range(4):
                rows.append(turned[g][40 * bs : 40 * bs + 40, 128 * o : 128 * o + 128])
        columns.append(jnp.concatenate(rows, axis=0))
    loads[5].wait()
    spectrum = dot(xback_ref[...], rhs3(jnp.concatenate(columns, axis=1)))
    for at, (b, o, s) in enumerate(ROWS):
        bs = b * ZP + s
        for parity in range(2):
            first = (o * 2 + parity) * HALF
            grid_ref[at * HALF : at * HALF + HALF, 128 * parity : 128 * parity + 128] = spectrum[
                first : first + HALF, 128 * bs : 128 * bs + 128
            ]
    high, low = split(grid_ref[:PART])
    left_ref[:PART] = high
    left_ref[PART:] = low

    id256 = lax.broadcasted_iota(jnp.int32, (256, 256), 0).astype(F32)
    zeros = jnp.zeros((2, 256), F32)

    def gather(pair):
        steps = (2 * pair, 2 * pair + 1)
        targets = [ahead_of(me, step) for step in steps]
        tiles = [first_ref[target, 0:8, :] for target in targets]
        x = jnp.concatenate([tile[6:7] for tile in tiles], axis=1)
        y = jnp.concatenate([tile[7:8] for tile in tiles], axis=1)
        x2 = jnp.floor(x * 0.5)
        here = id256[:HALF] == x2
        spot = (id256 == (x - 2.0 * x2) * 128.0 + y).astype(F32).astype(BF16)
        values = dot(left_ref[...], spot)
        rows = []
        for at in range(12):
            first = at * HALF
            one = values[first : first + HALF] + values[PART + first : PART + first + HALF]
            rows.append(jnp.sum(jnp.where(here, one, 0.0), axis=0, keepdims=True))
            if at % 6 == 5:
                rows.append(zeros)
        result = jnp.concatenate(rows, axis=0)
        for i in range(2):
            send2_ref[targets[i]] = result[:, 128 * i : 128 * i + 128]


    bytes_of(send_ref, N_FFT - 1, send_sems.at[0]).wait()
    send2_ref = send_ref

    def gather_group(at, carry):
        for i in range(UNROLL_G):
            gather(at * UNROLL_G + i)
        first = at * (2 * UNROLL_G)
        for i in range(1, 2 * UNROLL_G):
            put(send2_ref, last_ref, send_sems.at[1], send_sems.at[2], me, first + i).start()

        @pl.when(at > 0)
        def _():
            put(send2_ref, last_ref, send_sems.at[1], send_sems.at[2], me, first).start()

        return carry

    lax.fori_loop(0, N_FFT // 2 // UNROLL_G, gather_group, 0)
    own = pltpu.make_async_copy(send2_ref.at[me], last_ref.at[me], send_sems.at[2])
    own.start()

    for step in range(1, 4):
        source = lax.rem(group + 4 - step, 4)
        band_copy(
            mine_ref,
            total_ref.at[rows_of(source)],
            band_send_sems.at[2 + step],
            band_recv_sems.at[2 + step],
            source,
        ).wait_recv()
    for step in range(1, 4):
        share(step).wait_send()
    full_ref[...] = total_ref[...]

    bytes_of(last_ref, N_FFT, send_sems.at[2]).wait()
    land_ref[...] = last_ref[...]
    bytes_of(send2_ref, N_FFT - 1, send_sems.at[1]).wait()


def finish(
    stick_ref,
    land_ref,
    full_ref,
    core_ref,
    wave_ref,
    ztab_ref,
    out_ref,
    dens_ref,
    field_ref,
    box_ref,
    core3_ref,
):
    me = lax.axis_index("fft")
    for q in range(200):
        row = (q % 5) * 40 + q // 5
        core3_ref[:, row, :] = core_ref[:, 128 * q : 128 * q + 128]
    density = full_ref[:600].reshape(ZP, 200, 128)
    box_ref[...] = density
    for q in range(200):
        row = (q % 5) * 40 + q // 5
        dens_ref[:, 128 * q : 128 * q + 128] = box_ref[:, row, :]
    slot = lax.broadcasted_iota(jnp.int32, (ZP, 200, 128), 0)
    field = -lda_factor * jnp.exp(jnp.log(density + core3_ref[...]) * (1.0 / 3.0))
    core3_ref[...] = jnp.where(slot * N_FFT + me < N, field, 0.0)
    for q in range(200):
        row = (q % 5) * 40 + q // 5
        field_ref[:, 128 * q : 128 * q + 128] = core3_ref[:, row, :]
    x, y = grid_xy(stick_ref)
    half = N // 2
    x = jnp.where(x < half, x, x - N) / N
    y = jnp.where(y < half, y, y - N) / N
    g = lax.broadcasted_iota(jnp.int32, (N, 128), 0)
    z = jnp.where(g < half, g, g - N).astype(F32) / N
    kinetic = 2.0 * (x * x + y * y) + 2.0 * (z * z)
    both = [land_ref[:, 8 * b : 8 * b + 8, :].reshape(N_FFT * 8, 128) for b in range(2)]
    result = dot(ztab_ref[...], rhs3(jnp.concatenate(both, axis=1)))
    for o in range(2):
        for b in range(2):
            spectrum = result[N * o : N * o + N, 128 * b : 128 * b + 128]
            out_ref[o, b] = spectrum + kinetic * wave_ref[o, b]


VMEM = pltpu.VMEM
DMA = pltpu.SemaphoreType.DMA
SMEM_SPEC = pl.BlockSpec(memory_space=pltpu.SMEM)
VMEM_SPEC = pl.BlockSpec(memory_space=pltpu.VMEM)
ANY_SPEC = pl.BlockSpec(memory_space=pl.ANY)
LIMIT = 56 * 1024 * 1024


def call(body, in_specs, outs, scratch=(), flops=0, size=0, remote=None):
    options = {} if remote is None else dict(collective_id=remote, has_side_effects=True)
    return pl.pallas_call(
        body,
        out_shape=outs,
        in_specs=in_specs,
        out_specs=jax.tree.map(lambda _: VMEM_SPEC, outs),
        scratch_shapes=list(scratch),
        compiler_params=pltpu.CompilerParams(vmem_limit_bytes=LIMIT, **options),
        cost_estimate=pl.CostEstimate(flops=flops, bytes_accessed=size, transcendentals=0),
    )


def shape(*dims):
    return jax.ShapeDtypeStruct(dims, F32)


def make_calls():
    ytab = VMEM((8, 2, 256, 256), BF16)
    tiles = VMEM((N_FFT, 16, 128), F32)
    block = VMEM((64, 128), F32)
    big = call(
        whole,
        [SMEM_SPEC] * 3 + [VMEM_SPEC] * 5 + [ANY_SPEC] * 7,
        (shape(N_FFT, 16, 128), shape(4 * SLICE, 128)),
        (
            VMEM((2, 2, N, 128), F32),
            VMEM((8 * N_FFT, 6 * N), BF16),
            VMEM((2 * N, 12 * HALF), BF16),
            ytab,
            VMEM((NBLK, 64, 128), F32),
            VMEM((4 * HALF, 6 * N), BF16),
            ytab,
            tiles,
            tiles,
            tiles,
            VMEM((2 * PART, 256), F32),
            VMEM((4, 240, 256), F32),
            VMEM((4, 600, 128), F32),
            VMEM((4 * SLICE, 128), F32),
            VMEM((4 * NBLK, 128), F32),
            block,
            block,
            block,
            VMEM((128, 64, 128), F32),
            VMEM((ZP, 200, 128), F32),
            VMEM((4, NBLK, 128), F32),
            VMEM((4, 600, 128), F32),
            VMEM((2 * PART, 256), BF16),
            VMEM((3, SLICE, 128), F32),
            VMEM((SLICE, 128), F32),
            VMEM((4 * SLICE, 128), F32),
            DMA((7,)),
            DMA((3,)),
            DMA((N_FFT // CHUNK,)),
            DMA((2,)),
            DMA((2,)),
            DMA((6,)),
            DMA((6,)),
        ),
        20_000_000_000,
        16_000_000,
        0,
    )
    last = call(
        finish,
        [VMEM_SPEC] * 6,
        (shape(2, 2, N, 128), shape(ZP, N * N), shape(ZP, N * N)),
        (VMEM((ZP, 200, 128), F32), VMEM((ZP, 200, 128), F32)),
        500_000_000,
        4_000_000,
    )
    return big, last


def local(
    tables,
    wave_coef,
    stick_map,
    local_potential,
    core_density,
    occupations,
    block_place,
    block_atom,
    projectors,
    coupling,
):
    big, last = make_calls()
    stick_row = stick_map.reshape(1, 128)
    land, full = big(
        occupations,
        block_place,
        block_atom,
        block_place.reshape(1, NBLK),
        block_atom.reshape(1, NBLK),
        stick_row,
        coupling,
        local_potential,
        wave_coef,
        tables["z_ahead"],
        tables["x_ahead"],
        tables["y_ahead"],
        projectors,
        tables["x_back"],
        tables["y_back"],
    )
    return last(stick_row, land, full, core_density, wave_coef, tables["z_back"])


def solution(mesh):
    tables = {name: jnp.asarray(value) for name, value in make_tables().items()}

    def run(*args):
        return local(tables, *args)

    return jax.shard_map(
        run,
        mesh=mesh,
        in_specs=(
            P(None, "band", None, "fft"),
            P("fft"),
            P("fft", None),
            P("fft", None),
            P("band"),
            P("fft"),
            P("fft"),
            P("fft", None, None),
            P(),
        ),
        out_specs=(P(None, "band", None, "fft"), P("fft", None), P("fft", None)),
        check_vma=False,
    )
```

```python
import math

import jax
import jax.numpy as jnp
import numpy as np
from jax import lax
from jax.experimental import pallas as pl
from jax.experimental.pallas import tpu as pltpu
from jax.sharding import PartitionSpec as P

N = 160
ZP = 3
N_FFT = 64
NBLK = 96
ATOM_DEV = 16
ATOMS = 1024
BANDS_AXIS = 4
SLICE = 152
SHIFT = 52
BOX = 104
HALF = 56
F32 = jnp.float32
BF16 = jnp.bfloat16

lda_factor = (3.0 / math.pi) ** (1.0 / 3.0)


def parts(table):
    high = table.astype(np.float32).astype(jnp.bfloat16)
    low = (table - high.astype(np.float64)).astype(np.float32).astype(jnp.bfloat16)
    return high, low


def real_form(cosine, sine):
    return np.block([[cosine, -sine], [sine, cosine]])


def z_tables():
    slot, place = np.meshgrid(np.arange(8), np.arange(N_FFT), indexing="ij")
    out = np.zeros((N_FFT, 8, 2, N))
    g = np.arange(N)
    for f in range(N_FFT):
        for s in range(ZP):
            z = s * N_FFT + f
            if z < N:
                phase = 2 * np.pi / N * ((z * g) % N)
                c, d = np.cos(phase) / math.sqrt(N), np.sin(phase) / math.sqrt(N)
                out[f, s, 0], out[f, s, 1] = c, -d
                out[f, 3 + s, 0], out[f, 3 + s, 1] = d, c
    forward = out.reshape(N_FFT * 8, 2 * N)
    return forward, forward.T


def x_tables():
    rows = np.array([4 * k + g for g in range(4) for k in range(40)])
    compact = np.array([2 * h + p for p in range(2) for h in range(HALF)])
    phase = 2 * np.pi / N * ((rows[:, None] * (compact[None, :] - SHIFT)) % N)
    keep = (compact < BOX)[None, :] / math.sqrt(N)
    ahead = real_form(np.cos(phase) * keep, np.sin(phase) * keep)
    phase = phase.T
    keep = keep.T
    back = real_form(np.cos(phase) * keep, -np.sin(phase) * keep)
    return ahead, back


PAIRS = tuple((j, g) for g in range(4) for j in (g, g + 1))


def y_tables():
    compact = np.arange(128)
    out = []
    for j, g in PAIRS:
        flat = 128 * j + np.arange(128)
        keep = ((flat // N == g)[None, :] & (compact < BOX)[:, None]) / math.sqrt(N)
        phase = 2 * np.pi / N * (((compact[:, None] - SHIFT) * (flat % N)[None, :]) % N)
        c, d = np.cos(phase) * keep, np.sin(phase) * keep
        out.append(np.block([[c, d], [-d, c]]))
    return np.stack(out)


def stack3(table, axis):
    high, low = parts(table)
    return np.concatenate([high, low, high], axis=axis)


def make_tables():
    z_ahead, z_back = z_tables()
    x_ahead, x_back = x_tables()
    y_ahead = y_tables()
    y_back = np.swapaxes(y_ahead, 1, 2)
    return dict(
        z_ahead=stack3(z_ahead, 1),
        z_back=stack3(z_back, 1),
        x_ahead=stack3(x_ahead, 1),
        x_back=stack3(x_back, 1),
        y_ahead=np.stack(parts(y_ahead), axis=1),
        y_back=np.stack(parts(y_back), axis=1),
    )


def split(value):
    high = value.astype(BF16)
    return high, (value - high.astype(F32)).astype(BF16)


def dot(left, right):
    return lax.dot_general(left, right, (((1,), (0,)), ((), ())), preferred_element_type=F32)


def dot_nt(left, right):
    return lax.dot_general(left, right, (((1,), (1,)), ((), ())), preferred_element_type=F32)


def lhs3(value):
    high, low = split(value)
    return jnp.concatenate([high, high, low], axis=1)


def rhs3(value):
    high, low = split(value)
    return jnp.concatenate([high, high, low], axis=0)


def grid_xy(stick_ref):
    column = stick_ref[...].astype(F32)
    x = jnp.floor((column + 0.5) * (1.0 / N))
    y = column - N * x
    return x, y


def block_row(place):
    slot = (place >= 200).astype(jnp.int32) + (place >= 400).astype(jnp.int32)
    inside = place - 200 * slot
    fifth = (inside * 6554) >> 15
    return slot * 200 + (inside - 5 * fifth) * 40 + fifth


ROWS = [(b, o, s) for b in range(2) for o in range(2) for s in range(ZP)]
CHUNK = 4
UNROLL_S = 4
UNROLL_G = 4
PART = 12 * HALF


def ahead_of(me, step):
    return lax.rem(me + step, N_FFT)


def behind(me, step):
    return lax.rem(me + N_FFT - step, N_FFT)


def fft_copy(source, target, send_sem, recv_sem, device):
    return pltpu.make_async_remote_copy(
        src_ref=source,
        dst_ref=target,
        send_sem=send_sem,
        recv_sem=recv_sem,
        device_id={"fft": device},
        device_id_type=pl.DeviceIdType.MESH,
    )


def band_copy(source, target, send_sem, recv_sem, device):
    return pltpu.make_async_remote_copy(
        src_ref=source,
        dst_ref=target,
        send_sem=send_sem,
        recv_sem=recv_sem,
        device_id={"band": device},
        device_id_type=pl.DeviceIdType.MESH,
    )


def put(send_ref, land_ref, send_sem, recv_sem, me, step):
    target = ahead_of(me, step)
    return fft_copy(send_ref.at[target], land_ref.at[me], send_sem, recv_sem, target)


def bytes_of(ref, count, sem):
    return pltpu.make_async_copy(ref.at[pl.ds(0, count)], ref.at[pl.ds(0, count)], sem)


def whole(
    occ_ref,
    place_ref,
    atom_ref,
    place_row_ref,
    atom_row_ref,
    stick_ref,
    coupling_ref,
    potential_ref,
    wave_hbm,
    ztab_hbm,
    xtab_hbm,
    ytab_hbm,
    proj_hbm,
    xback_hbm,
    yback_hbm,
    land_ref,
    full_ref,
    wave_ref,
    ztab_ref,
    xtab_ref,
    ytab_ref,
    proj_ref,
    xback_ref,
    yback_ref,
    send_ref,
    first_ref,
    last_ref,
    grid_ref,
    mid_ref,
    psi_ref,
    power_ref,
    piece_ref,
    sums_ref,
    before_ref,
    after_ref,
    weight_ref,
    pot_ref,
    add_ref,
    h_ref,
    left_ref,
    part_ref,
    mine_ref,
    total_ref,
    sems,
    send_sems,
    recv_sems,
    halo_send_sems,
    halo_recv_sems,
    band_send_sems,
    band_recv_sems,
):
    me = lax.axis_index("fft")
    group = lax.axis_index("band")
    barrier = pltpu.get_barrier_semaphore()
    loads = [
        pltpu.make_async_copy(source, target, sems.at[i])
        for i, (source, target) in enumerate(
            [
                (wave_hbm, wave_ref),
                (ztab_hbm, ztab_ref),
                (xtab_hbm, xtab_ref),
                (ytab_hbm, ytab_ref),
                (proj_hbm, proj_ref),
                (xback_hbm, xback_ref),
                (yback_hbm, yback_ref),
            ]
        )
    ]
    for load in loads:
        load.start()

    def greet(step, carry):
        pl.semaphore_signal(
            barrier,
            inc=1,
            device_id={"fft": ahead_of(me, step)},
            device_id_type=pl.DeviceIdType.MESH,
        )
        return carry

    lax.fori_loop(1, N_FFT, greet, 0, unroll=3)
    for step in range(1, 4):
        pl.semaphore_signal(
            barrier,
            inc=1,
            device_id={"band": lax.rem(group + step, 4)},
            device_id_type=pl.DeviceIdType.MESH,
        )

    grid_ref[...] = jnp.zeros_like(grid_ref)
    x, y = grid_xy(stick_ref)
    half = N // 2
    xc = jnp.where(x < half, x, x - N) + SHIFT
    yc = jnp.where(y < half, y, y - N) + SHIFT
    loads[0].wait()
    loads[1].wait()
    both = [jnp.concatenate([wave_ref[0, b], wave_ref[1, b]], axis=0) for b in range(2)]
    result = dot(ztab_ref[...], rhs3(jnp.concatenate(both, axis=1)))
    for b in range(2):
        send_ref[:, 8 * b : 8 * b + 8, :] = result[:, 128 * b : 128 * b + 128].reshape(
            N_FFT, 8, 128
        )
    send_ref[:, 6:7, :] = jnp.broadcast_to(xc[None], (N_FFT, 1, 128))
    send_ref[:, 7:8, :] = jnp.broadcast_to(yc[None], (N_FFT, 1, 128))

    pl.semaphore_wait(barrier, N_FFT - 1 + 3)

    def send(step, carry):
        chunk = lax.div(step, CHUNK)
        put(send_ref, first_ref, send_sems.at[0], recv_sems.at[chunk], me, step).start()
        return carry

    lax.fori_loop(1, N_FFT, send, 0, unroll=3)
    pltpu.make_async_copy(send_ref.at[me], first_ref.at[me], recv_sems.at[0]).start()

    row_id = lax.broadcasted_iota(jnp.int32, (HALF, 128), 0).astype(F32)
    lane_id = lax.broadcasted_iota(jnp.int32, (256, 128), 0).astype(F32)

    def scatter(chunk):
        lefts, rights = [], []
        for i in range(CHUNK):
            step = chunk * CHUNK + i
            tile = first_ref[behind(me, step)]
            x, y = tile[6:7], tile[7:8]
            x2 = jnp.floor(x * 0.5)
            here = row_id == x2
            rights.append((lane_id == (x - 2.0 * x2) * 128.0 + y).astype(F32).astype(BF16))
            high = tile.astype(BF16).astype(F32)
            picked = [
                jnp.where(here, piece[8 * b + 3 * o + s : 8 * b + 3 * o + s + 1], 0.0)
                for piece in (high, tile - high)
                for b, o, s in ROWS
            ]
            lefts.append(jnp.concatenate(picked, axis=0).astype(BF16))
        grid_ref[...] += dot_nt(jnp.concatenate(lefts, axis=1), jnp.concatenate(rights, axis=1))

    def scatter_group(at, carry):
        for i in range(UNROLL_S):
            bytes_of(first_ref, CHUNK, recv_sems.at[at * UNROLL_S + i]).wait()
        for i in range(UNROLL_S):
            scatter(at * UNROLL_S + i)
        return carry

    lax.fori_loop(0, N_FFT // CHUNK // UNROLL_S, scatter_group, 0)

    columns = []
    for b in range(2):
        for s in range(ZP):
            rows = []
            for o in range(2):
                first = (b * 6 + o * 3 + s) * HALF
                for parity in range(2):
                    lanes = slice(128 * parity, 128 * parity + 128)
                    rows.append(
                        grid_ref[first : first + HALF, lanes]
                        + grid_ref[PART + first : PART + first + HALF, lanes]
                    )
            columns.append(jnp.concatenate(rows, axis=0))
    loads[2].wait()
    mixed = dot(xtab_ref[...], rhs3(jnp.concatenate(columns, axis=1)))
    for g in range(4):
        for o in range(2):
            first = (o * 4 + g) * 40
            for bs in range(6):
                mid_ref[g, 40 * bs : 40 * bs + 40, 128 * o : 128 * o + 128] = mixed[
                    first : first + 40, 128 * bs : 128 * bs + 128
                ]
    lefts = [lhs3(mid_ref[g]) for g in range(4)]
    loads[3].wait()
    for j in range(5):
        total = None
        for at, (tile, g) in enumerate(PAIRS):
            if tile == j:
                high, low = ytab_ref[at, 0], ytab_ref[at, 1]
                term = dot(lefts[g], jnp.concatenate([high, low, high], axis=0))
                total = term if total is None else total + term
        for b in range(2):
            for s in range(ZP):
                bs = b * ZP + s
                for o in range(2):
                    first = s * 200 + j * 40
                    psi_ref[b * 2 + o, first : first + 40, :] = total[
                        40 * bs : 40 * bs + 40, 128 * o : 128 * o + 128
                    ]

    def power(b):
        re, im = psi_ref[2 * b], psi_ref[2 * b + 1]
        return re * re + im * im

    power_ref[:600] = occ_ref[0] * power(0) + occ_ref[1] * power(1)
    power_ref[600:] = jnp.zeros((4 * SLICE - 600, 128), F32)

    def rows_of(index):
        return pl.ds(pl.multiple_of(index * SLICE, 8), SLICE)

    def quarter(step):
        target = lax.rem(group + step, 4)
        return band_copy(
            power_ref.at[rows_of(target)],
            part_ref.at[step - 1],
            band_send_sems.at[step - 1],
            band_recv_sems.at[step - 1],
            target,
        )

    for step in range(1, 4):
        quarter(step).start()

    def fetch(k, carry):
        row = block_row(place_ref[k])
        for c in range(4):
            piece_ref[pl.ds(4 * k + c, 1), :] = psi_ref[c, pl.ds(row, 1), :]
        return carry

    lax.fori_loop(0, NBLK, fetch, 0, unroll=2)
    loads[4].wait()
    lane = lax.broadcasted_iota(jnp.int32, (64, 128), 1)
    picks = []
    for part in range(3):
        piece_high, piece_low = split(piece_ref[128 * part : 128 * part + 128])
        piece_both = jnp.concatenate([piece_high, piece_high], axis=1)
        found = jnp.zeros((64, 128), F32)
        for chunk in range(2):
            first = part * 32 + chunk * 16
            high, low = split(proj_ref[first : first + 16].reshape(1024, 128))
            values = dot_nt(jnp.concatenate([high, low], axis=1), piece_both)
            values = values + dot_nt(high, piece_low)
            for m in range(16):
                own = lax.div(lane, 4) == chunk * 16 + m
                found = jnp.where(own, values[64 * m : 64 * m + 64], found)
        picks.append(found)
    found = jnp.concatenate(picks, axis=1)
    base = me * ATOM_DEV - ATOM_DEV // 2
    near = lax.rem(atom_row_ref[...] - base + 2 * ATOMS, ATOMS).astype(F32)
    spread = lax.div(lax.broadcasted_iota(jnp.int32, (NBLK, 4 * NBLK), 1), 4)
    spread = spread == lax.broadcasted_iota(jnp.int32, (NBLK, 4 * NBLK), 0)
    near = dot(
        jnp.broadcast_to(near, (16, NBLK)).astype(BF16), spread.astype(F32).astype(BF16)
    )[0:1]
    column = lax.broadcasted_iota(jnp.int32, (128, 4 * NBLK), 0)
    owner = lax.rem(lax.broadcasted_iota(jnp.int32, (128, 4 * NBLK), 1), 4).astype(F32) + 4.0 * near
    member = (owner == column.astype(F32)).astype(F32).astype(BF16)
    high, low = split(found)
    sums_ref[...] = dot_nt(
        jnp.concatenate([high, low], axis=1), jnp.concatenate([member, member], axis=1)
    )
    after_me, before_me = ahead_of(me, 1), behind(me, 1)
    to_after = fft_copy(
        sums_ref, before_ref, halo_send_sems.at[0], halo_recv_sems.at[0], after_me
    )
    to_before = fft_copy(
        sums_ref, after_ref, halo_send_sems.at[1], halo_recv_sems.at[1], before_me
    )
    to_after.start()
    to_before.start()

    for q in range(200):
        row = (q % 5) * 40 + q // 5
        pot_ref[:, row, :] = potential_ref[:, 128 * q : 128 * q + 128]

    for step in range(1, 4):
        quarter(step).wait()
    mine_ref[...] = power_ref[rows_of(group)] + part_ref[0] + part_ref[1] + part_ref[2]
    total_ref[rows_of(group)] = mine_ref[...]

    def share(step):
        return band_copy(
            mine_ref,
            total_ref.at[rows_of(group)],
            band_send_sems.at[2 + step],
            band_recv_sems.at[2 + step],
            lax.rem(group + step, 4),
        )

    for step in range(1, 4):
        share(step).start()

    to_after.wait()
    to_before.wait()
    beside = jnp.where(
        lane < 64, pltpu.roll(before_ref[...], 64, 1), pltpu.roll(after_ref[...], 64, 1)
    )
    weight = lax.dot_general(
        coupling_ref[...],
        sums_ref[...] + beside,
        (((1,), (0,)), ((), ())),
        precision=lax.Precision.HIGHEST,
        preferred_element_type=F32,
    )
    for n in range(128):
        weight_ref[n] = jnp.broadcast_to(weight[:, n : n + 1], (64, 128))

    def added(k, carry):
        first = ((atom_ref[k] - base) & (2 * ATOM_DEV - 1)) * 4
        values = proj_ref[k]
        for c in range(4):
            add_ref[c, pl.ds(k, 1), :] = jnp.sum(
                values * weight_ref[first + c], axis=0, keepdims=True
            )
        return carry

    lax.fori_loop(0, NBLK, added, 0, unroll=2)
    place = place_row_ref[...]
    slot = (place >= 200).astype(jnp.int32) + (place >= 400).astype(jnp.int32)
    inside = place - 200 * slot
    fifth = (inside * 6554) >> 15
    place = slot * 200 + (inside - 5 * fifth) * 40 + fifth
    block_id = lax.broadcasted_iota(jnp.int32, (600, NBLK), 0)
    spot = (block_id == place).astype(F32).astype(BF16)
    potential = pot_ref[...].reshape(600, 128)
    for c in range(4):
        high, low = split(add_ref[c])
        h_ref[c] = potential * psi_ref[c] + (dot(spot, high) + dot(spot, low))

    lefts = []
    for j in range(5):
        rows = []
        for b in range(2):
            for s in range(ZP):
                first = s * 200 + j * 40
                rows.append(
                    jnp.concatenate(
                        [h_ref[b * 2 + o, first : first + 40, :] for o in range(2)], axis=1
                    )
                )
        lefts.append(lhs3(jnp.concatenate(rows, axis=0)))
    loads[6].wait()
    turned = []
    for g in range(4):
        total = None
        for at, (j, owner) in enumerate(PAIRS):
            if owner == g:
                high, low = yback_ref[at, 0], yback_ref[at, 1]
                term = dot(lefts[j], jnp.concatenate([high, low, high], axis=0))
                total = term if total is None else total + term
        turned.append(total)
    columns = []
    for bs in range(6):
        rows = []
        for o in range(2):
            for g in range(4):
                rows.append(turned[g][40 * bs : 40 * bs + 40, 128 * o : 128 * o + 128])
        columns.append(jnp.concatenate(rows, axis=0))
    loads[5].wait()
    spectrum = dot(xback_ref[...], rhs3(jnp.concatenate(columns, axis=1)))
    for at, (b, o, s) in enumerate(ROWS):
        bs = b * ZP + s
        for parity in range(2):
            first = (o * 2 + parity) * HALF
            grid_ref[at * HALF : at * HALF + HALF, 128 * parity : 128 * parity + 128] = spectrum[
                first : first + HALF, 128 * bs : 128 * bs + 128
            ]
    high, low = split(grid_ref[:PART])
    left_ref[:PART] = high
    left_ref[PART:] = low

    id256 = lax.broadcasted_iota(jnp.int32, (256, 256), 0).astype(F32)
    zeros = jnp.zeros((2, 256), F32)

    def gather(pair):
        steps = (2 * pair, 2 * pair + 1)
        targets = [ahead_of(me, step) for step in steps]
        tiles = [first_ref[target, 0:8, :] for target in targets]
        x = jnp.concatenate([tile[6:7] for tile in tiles], axis=1)
        y = jnp.concatenate([tile[7:8] for tile in tiles], axis=1)
        x2 = jnp.floor(x * 0.5)
        here = id256[:HALF] == x2
        spot = (id256 == (x - 2.0 * x2) * 128.0 + y).astype(F32).astype(BF16)
        values = dot(left_ref[...], spot)
        rows = []
        for at in range(12):
            first = at * HALF
            one = values[first : first + HALF] + values[PART + first : PART + first + HALF]
            rows.append(jnp.sum(jnp.where(here, one, 0.0), axis=0, keepdims=True))
            if at % 6 == 5:
                rows.append(zeros)
        result = jnp.concatenate(rows, axis=0)
        for i in range(2):
            send2_ref[targets[i]] = result[:, 128 * i : 128 * i + 128]


    bytes_of(send_ref, N_FFT - 1, send_sems.at[0]).wait()
    send2_ref = send_ref

    def gather_group(at, carry):
        for i in range(UNROLL_G):
            gather(at * UNROLL_G + i)
        first = at * (2 * UNROLL_G)
        for i in range(1, 2 * UNROLL_G):
            put(send2_ref, last_ref, send_sems.at[1], send_sems.at[2], me, first + i).start()

        @pl.when(at > 0)
        def _():
            put(send2_ref, last_ref, send_sems.at[1], send_sems.at[2], me, first).start()

        return carry

    lax.fori_loop(0, N_FFT // 2 // UNROLL_G, gather_group, 0)
    own = pltpu.make_async_copy(send2_ref.at[me], last_ref.at[me], send_sems.at[2])
    own.start()

    for step in range(1, 4):
        source = lax.rem(group + 4 - step, 4)
        band_copy(
            mine_ref,
            total_ref.at[rows_of(source)],
            band_send_sems.at[2 + step],
            band_recv_sems.at[2 + step],
            source,
        ).wait_recv()
    for step in range(1, 4):
        share(step).wait_send()
    full_ref[...] = total_ref[...]

    bytes_of(last_ref, N_FFT, send_sems.at[2]).wait()
    land_ref[...] = last_ref[...]
    bytes_of(send2_ref, N_FFT - 1, send_sems.at[1]).wait()


def finish(
    stick_ref,
    land_ref,
    full_ref,
    core_ref,
    wave_ref,
    ztab_ref,
    out_ref,
    dens_ref,
    field_ref,
    box_ref,
    core3_ref,
):
    me = lax.axis_index("fft")
    for q in range(200):
        row = (q % 5) * 40 + q // 5
        core3_ref[:, row, :] = core_ref[:, 128 * q : 128 * q + 128]
    density = full_ref[:600].reshape(ZP, 200, 128)
    box_ref[...] = density
    for q in range(200):
        row = (q % 5) * 40 + q // 5
        dens_ref[:, 128 * q : 128 * q + 128] = box_ref[:, row, :]
    slot = lax.broadcasted_iota(jnp.int32, (ZP, 200, 128), 0)
    field = -lda_factor * jnp.exp(jnp.log(density + core3_ref[...]) * (1.0 / 3.0))
    core3_ref[...] = jnp.where(slot * N_FFT + me < N, field, 0.0)
    for q in range(200):
        row = (q % 5) * 40 + q // 5
        field_ref[:, 128 * q : 128 * q + 128] = core3_ref[:, row, :]
    x, y = grid_xy(stick_ref)
    half = N // 2
    x = jnp.where(x < half, x, x - N) / N
    y = jnp.where(y < half, y, y - N) / N
    g = lax.broadcasted_iota(jnp.int32, (N, 128), 0)
    z = jnp.where(g < half, g, g - N).astype(F32) / N
    kinetic = 2.0 * (x * x + y * y) + 2.0 * (z * z)
    both = [land_ref[:, 8 * b : 8 * b + 8, :].reshape(N_FFT * 8, 128) for b in range(2)]
    result = dot(ztab_ref[...], rhs3(jnp.concatenate(both, axis=1)))
    for o in range(2):
        for b in range(2):
            spectrum = result[N * o : N * o + N, 128 * b : 128 * b + 128]
            out_ref[o, b] = spectrum + kinetic * wave_ref[o, b]


VMEM = pltpu.VMEM
DMA = pltpu.SemaphoreType.DMA
SMEM_SPEC = pl.BlockSpec(memory_space=pltpu.SMEM)
VMEM_SPEC = pl.BlockSpec(memory_space=pltpu.VMEM)
ANY_SPEC = pl.BlockSpec(memory_space=pl.ANY)
LIMIT = 56 * 1024 * 1024


def call(body, in_specs, outs, scratch=(), flops=0, size=0, remote=None):
    options = {} if remote is None else dict(collective_id=remote, has_side_effects=True)
    return pl.pallas_call(
        body,
        out_shape=outs,
        in_specs=in_specs,
        out_specs=jax.tree.map(lambda _: VMEM_SPEC, outs),
        scratch_shapes=list(scratch),
        compiler_params=pltpu.CompilerParams(vmem_limit_bytes=LIMIT, **options),
        cost_estimate=pl.CostEstimate(flops=flops, bytes_accessed=size, transcendentals=0),
    )


def shape(*dims):
    return jax.ShapeDtypeStruct(dims, F32)


def make_calls():
    ytab = VMEM((8, 2, 256, 256), BF16)
    tiles = VMEM((N_FFT, 16, 128), F32)
    block = VMEM((64, 128), F32)
    big = call(
        whole,
        [SMEM_SPEC] * 3 + [VMEM_SPEC] * 5 + [ANY_SPEC] * 7,
        (shape(N_FFT, 16, 128), shape(4 * SLICE, 128)),
        (
            VMEM((2, 2, N, 128), F32),
            VMEM((8 * N_FFT, 6 * N), BF16),
            VMEM((2 * N, 12 * HALF), BF16),
            ytab,
            VMEM((NBLK, 64, 128), F32),
            VMEM((4 * HALF, 6 * N), BF16),
            ytab,
            tiles,
            tiles,
            tiles,
            VMEM((2 * PART, 256), F32),
            VMEM((4, 240, 256), F32),
            VMEM((4, 600, 128), F32),
            VMEM((4 * SLICE, 128), F32),
            VMEM((4 * NBLK, 128), F32),
            block,
            block,
            block,
            VMEM((128, 64, 128), F32),
            VMEM((ZP, 200, 128), F32),
            VMEM((4, NBLK, 128), F32),
            VMEM((4, 600, 128), F32),
            VMEM((2 * PART, 256), BF16),
            VMEM((3, SLICE, 128), F32),
            VMEM((SLICE, 128), F32),
            VMEM((4 * SLICE, 128), F32),
            DMA((7,)),
            DMA((3,)),
            DMA((N_FFT // CHUNK,)),
            DMA((2,)),
            DMA((2,)),
            DMA((6,)),
            DMA((6,)),
        ),
        20_000_000_000,
        16_000_000,
        0,
    )
    last = call(
        finish,
        [VMEM_SPEC] * 6,
        (shape(2, 2, N, 128), shape(ZP, N * N), shape(ZP, N * N)),
        (VMEM((ZP, 200, 128), F32), VMEM((ZP, 200, 128), F32)),
        500_000_000,
        4_000_000,
    )
    return big, last


def local(
    tables,
    wave_coef,
    stick_map,
    local_potential,
    core_density,
    occupations,
    block_place,
    block_atom,
    projectors,
    coupling,
):
    big, last = make_calls()
    stick_row = stick_map.reshape(1, 128)
    land, full = big(
        occupations,
        block_place,
        block_atom,
        block_place.reshape(1, NBLK),
        block_atom.reshape(1, NBLK),
        stick_row,
        coupling,
        local_potential,
        wave_coef,
        tables["z_ahead"],
        tables["x_ahead"],
        tables["y_ahead"],
        projectors,
        tables["x_back"],
        tables["y_back"],
    )
    return last(stick_row, land, full, core_density, wave_coef, tables["z_back"])


def solution(mesh):
    tables = {name: jnp.asarray(value) for name, value in make_tables().items()}

    def run(*args):
        return local(tables, *args)

    return jax.shard_map(
        run,
        mesh=mesh,
        in_specs=(
            P(None, "band", None, "fft"),
            P("fft"),
            P("fft", None),
            P("fft", None),
            P("band"),
            P("fft"),
            P("fft"),
            P("fft", None, None),
            P(),
        ),
        out_specs=(P(None, "band", None, "fft"), P("fft", None), P("fft", None)),
        check_vma=False,
    )
```
